32 devices in a mesh: dp: 2 (over x), section: 4 (over z), space: 4 (over y, core).
Axes of the slice: x: 2, y: 2, z: 4, core: 2. Of those that a mesh axis runs over, the one named last changes fastest.
Arguments:
- images: bfloat16 [4, 4, 64, 256], P('dp', 'space'), may hold values from -6 to 6
- steps: int32 [4], P('dp'), may hold values from 0 to 999
- out_grad: bfloat16 [4, 4, 64, 256], P('dp', 'space'), may hold values from -0.5 to 0.5
- conv_weight: bfloat16 [4, 3, 3, 256, 256], P('section'), may hold values from -0.125 to 0.125
- gn_gain: float32 [4, 256], P('section'), may hold values from 0.5 to 2
- emb_weight: bfloat16 [4, 256, 512], P('section'), may hold values from -0.375 to 0.375
Outputs:
- grad_conv: float32 [4, 3, 3, 256, 256], P('section')
- grad_gain: float32 [4, 256], P('section')
- grad_emb: float32 [4, 256, 512], P('section')
The draws below stay inside these ranges and needn't reach their ends.
All inputs are finite; a program needn't handle non-finite values.
Results may differ from the reference program's by a relative error of at most 0.0064.
Values may be sent and summed in bfloat16 or wider, within the bound.
A program may use at most 64 MiB of HBM per device.

```python
import math
import jax
import jax.numpy as jnp
from jax import lax

C = 256
G = 32
FREQ = 256
MICRO = 2
IMGS = 1
COLS = 64
SECTIONS = 4
BATCH = 4
H = 4
N_DP = 2


def touch_ends(values, rng, smallest, largest):
    place = [jax.random.randint(jax.random.fold_in(rng, axis), (), 0, length) for axis, length in enumerate(values.shape)]
    longest = values.shape.index(max(values.shape))
    next_to = place[:longest] + [(place[longest] + 1) % values.shape[longest]] + place[longest + 1:]
    return values.at[tuple(place)].set(smallest).at[tuple(next_to)].set(largest)


def shard_levels(key, dims, shards, smallest, top_value):
    def one(position, parts):
        draws = jax.random.uniform(jax.random.fold_in(jax.random.fold_in(key, 6), position), (parts,), jnp.float32, smallest / len(shards), top_value / len(shards))
        return jnp.repeat(jnp.exp(draws), dims[position] // parts).reshape((-1,) + (1,) * (len(dims) - position - 1))

    loudness = one(*shards[0])
    for cut in shards[1:]:
        loudness = loudness * one(*cut)
    return loudness


def scatter_about(key, dims, scale, limit, shards=(), held_as=jnp.bfloat16):
    entries = scale * jax.random.normal(key, dims, jnp.float32)
    if shards:
        entries = entries * shard_levels(key, dims, shards, -0.22, 0.18)
    return jnp.clip(entries, -limit, limit).astype(held_as)


def setup_inputs(seed: int = 0) -> dict:
    splits = jax.random.split(jax.random.key(seed), 7)
    return {
        "images": scatter_about(splits[0], (BATCH, H, COLS, C), 1.0, 6.0, ((0, 2), (1, 4))),
        "steps": touch_ends(jax.random.randint(splits[1], (BATCH,), 0, 1000), jax.random.fold_in(splits[1], 1), 0, 999).astype(jnp.int32),
        "out_grad": scatter_about(splits[2], (BATCH, H, COLS, C), ((BATCH * H * COLS) ** -0.5), 0.5, ((0, 2), (1, 4))),
        "conv_weight": scatter_about(splits[3], (SECTIONS, 3, 3, C, C), (9 * C) ** -0.5, 0.125, ((0, 4),)),
        "gn_gain": jnp.clip(jnp.exp(math.log(2.0) - 1.3862944 * jax.random.uniform(splits[4], (SECTIONS, C), jnp.float32) ** shard_levels(splits[4], (SECTIONS, C), ((0, 4),), -0.2, 0.2)), 0.5, 2.0),
        "emb_weight": scatter_about(splits[5], (SECTIONS, FREQ, 2 * C), FREQ ** -0.5, 0.375, ((0, 4),)),
    }


EPS = 1e-05

def sinusoid(timesteps, feature_n):
    half_n = feature_n // 2
    freqs = jnp.exp(-math.log(10000.0) * jnp.arange(half_n, dtype=jnp.float32) / half_n)
    angles = timesteps.astype(jnp.float32)[:, None] * freqs[None, :]
    return jnp.concatenate([jnp.cos(angles), jnp.sin(angles)], axis=1)

def group_sums(tensor, groups):
    batch_n, height_n, width_n, channels = tensor.shape
    split = tensor.reshape(batch_n, height_n, width_n, groups, channels // groups)
    return (lax.optimization_barrier(jnp.sum(split, axis=(1, 2, 4))), lax.optimization_barrier(jnp.sum(split * split, axis=(1, 2, 4))))

def spread(values, channels):
    return jnp.repeat(values, channels // values.shape[1], axis=1)[:, None, None, :]

def normalize(tensor, first_sum, square_sum, gains, scales, shifts, cell_count):
    channels = tensor.shape[3]
    average = first_sum / cell_count
    inverse = lax.rsqrt(square_sum / cell_count - average * average + EPS)
    normed = (tensor - spread(average, channels)) * spread(inverse, channels) * gains
    return normed * (1.0 + scales[:, None, None, :]) + shifts[:, None, None, :]

def patches(padded, height_n, width_n):
    return jnp.concatenate([padded[:, vertical:vertical + height_n, lateral:lateral + width_n, :] for vertical in range(3) for lateral in range(3)], axis=3)

def convolve(padded, matrix):
    batch_n, height_p, width_p, channels = padded.shape
    flat = patches(padded, height_p - 2, width_p - 2).reshape(-1, 9 * channels)
    return jnp.dot(flat, matrix, preferred_element_type=jnp.float32).reshape(batch_n, height_p - 2, width_p - 2, matrix.shape[1])

def flip_weight(weight):
    channels = weight.shape[2]
    return jnp.transpose(weight[::-1, ::-1], (0, 1, 3, 2)).reshape(9 * channels, channels)

def silu_slope(pre_act):
    sigmoid_v = jax.nn.sigmoid(pre_act)
    return sigmoid_v * (1.0 + pre_act * (1.0 - sigmoid_v))

def pad_both(tensor):
    return jnp.pad(tensor, ((0, 0), (1, 1), (1, 1), (0, 0)))

def norm_backward(tensor, first_sum, square_sum, gains, scales, shifts, cell_count, d_pre):

    def mapping(tensor_v, first_v, square_v, gains_v, scales_v, shifts_v):
        return normalize(tensor_v, first_v, square_v, gains_v, scales_v, shifts_v, cell_count)
    _, pull_back = jax.vjp(mapping, tensor, first_sum, square_sum, gains, scales, shifts)
    return pull_back(d_pre)

def block_forward(inputs, weight, gains, emb_matrix, features, cell_count):
    tensor = inputs.astype(jnp.float32)
    channels = tensor.shape[3]
    first_sum, square_sum = group_sums(tensor, G)
    embedded = jnp.dot(features, emb_matrix.astype(jnp.float32), precision=lax.Precision.HIGHEST)
    scales = embedded[:, :channels]
    shifts = embedded[:, channels:]
    pre_act = normalize(tensor, first_sum, square_sum, gains, scales, shifts, cell_count)
    activation = jax.nn.silu(pre_act).astype(jnp.bfloat16)
    padded = pad_both(activation)
    conv_out = convolve(padded, weight.reshape(9 * channels, channels))
    output = (tensor + conv_out).astype(jnp.bfloat16)
    return (output, (tensor, first_sum, square_sum, scales, shifts, pre_act, padded))

def block_backward(upstream, saved, weight, gains, cell_count):
    tensor, first_sum, square_sum, scales, shifts, pre_act, padded = saved
    batch_n, height_n, width_n, channels = tensor.shape
    flat_patch = patches(padded, height_n, width_n).reshape(-1, 9 * channels)
    d_weight = jnp.dot(flat_patch.T, upstream.reshape(-1, channels), preferred_element_type=jnp.float32)
    d_act = convolve(pad_both(upstream), flip_weight(weight))
    d_pre = d_act * silu_slope(pre_act)
    d_tensor, d_first, d_square, d_gains, d_scales, d_shifts = norm_backward(tensor, first_sum, square_sum, gains, scales, shifts, cell_count, d_pre)
    d_tensor = d_tensor + spread(d_first, channels) + 2.0 * tensor * spread(d_square, channels)
    d_input = (upstream.astype(jnp.float32) + d_tensor).astype(jnp.bfloat16)
    return (d_input, d_weight, d_gains, jnp.concatenate([d_scales, d_shifts], axis=1))

def reference(images, steps, out_grad, conv_weight, gn_gain, emb_weight):
    group_n = MICRO * IMGS
    shape = (N_DP, group_n, H, COLS, C)
    cell_count = H * COLS * (C // G)

    def one_group(totals, pieces):
        group_images, group_steps, group_grad = pieces
        features = sinusoid(group_steps, FREQ)
        stash = []
        current = group_images
        for section_no in range(SECTIONS - 1):
            current, saved = block_forward(current, conv_weight[section_no], gn_gain[section_no], emb_weight[section_no], features, cell_count)
            stash.append((current, saved))
        joined = (current.astype(jnp.float32) + stash[0][0].astype(jnp.float32)).astype(jnp.bfloat16)
        final_out, final_saved = block_forward(joined, conv_weight[3], gn_gain[3], emb_weight[3], features, cell_count)
        back_three = block_backward(group_grad, final_saved, conv_weight[3], gn_gain[3], cell_count)
        back_two = block_backward(back_three[0], stash[2][1], conv_weight[2], gn_gain[2], cell_count)
        back_one = block_backward(back_two[0], stash[1][1], conv_weight[1], gn_gain[1], cell_count)
        start_zero = (back_one[0].astype(jnp.float32) + back_three[0].astype(jnp.float32)).astype(jnp.bfloat16)
        back_zero = block_backward(start_zero, stash[0][1], conv_weight[0], gn_gain[0], cell_count)
        records = [back_zero, back_one, back_two, back_three]
        conv_sum = jnp.stack([record[1] for record in records]).reshape(SECTIONS, 3, 3, C, C)
        gain_sum = jnp.stack([record[2] for record in records])
        emb_sum = jnp.stack([jnp.dot(features.T, record[3], precision=lax.Precision.HIGHEST) for record in records])
        return ((totals[0] + conv_sum, totals[1] + gain_sum, totals[2] + emb_sum), None)
    start = (jnp.zeros((SECTIONS, 3, 3, C, C), jnp.float32), jnp.zeros((SECTIONS, C), jnp.float32), jnp.zeros((SECTIONS, FREQ, 2 * C), jnp.float32))
    totals, _ = lax.scan(one_group, start, (images.reshape(shape), steps.reshape(N_DP, group_n), out_grad.reshape(shape)))
    return (totals[0], totals[1], totals[2])
```

```python
import functools
import math

import jax
import jax.numpy as jnp
import numpy as np
from jax import lax
from jax.experimental import pallas as pl
from jax.experimental.pallas import tpu as pltpu
from jax.sharding import PartitionSpec as P

G = 32
EPS = 1e-05
MESH = pl.DeviceIdType.MESH
F32 = jnp.float32
BF16 = jnp.bfloat16
PIX = 256
COLS = 64
C = 256


def thirds(x):
    first = x.astype(BF16)
    rest = x - first.astype(F32)
    second = rest.astype(BF16)
    return first, second, (rest - second.astype(F32)).astype(BF16)


def exact_dot(x, matrix):
    parts = [jnp.dot(part, matrix, preferred_element_type=F32) for part in thirds(x)]
    return parts[0] + (parts[1] + parts[2])


def rows_of(*rows):
    index = lax.broadcasted_iota(jnp.int32, (8, rows[0].shape[1]), 0)
    out = jnp.zeros((8, rows[0].shape[1]), F32)
    for i, row in enumerate(rows):
        out = jnp.where(index == i, row, out)
    return out


def spread_columns(ref, value):
    column = lax.broadcasted_iota(jnp.int32, (PIX, C), 0) & (COLS - 1)
    left = jnp.where(column == 0, 0.0, pltpu.roll(value, 1, 0))
    right = jnp.where(column == COLS - 1, 0.0, pltpu.roll(value, PIX - 1, 0))
    ref[COLS : COLS + PIX, 0:C] = left.astype(BF16)
    ref[COLS : COLS + PIX, C : 2 * C] = value.astype(BF16)
    ref[COLS : COLS + PIX, 2 * C : 3 * C] = right.astype(BF16)


def clear_border(ref):
    blank = jnp.zeros((COLS, 3 * C), BF16)
    ref[0:COLS, :] = blank
    ref[COLS + PIX : 2 * COLS + PIX, :] = blank


def convolve(ref, kernel_of):
    total = None
    for ky in range(3):
        part = jnp.dot(
            ref[ky * COLS : ky * COLS + PIX, :], kernel_of(ky), preferred_element_type=F32
        )
        total = part if total is None else total + part
    return total


def body(
    n_sec, flips, steps, freqs, images, out_grad, weight, gain, emb,
    conv_out, gain_out, emb_out,
    hbuf, skip, gskip, obuf, dbuf, act_t, g_all, small, turned, act_cols, g_cols,
    normed, slope, d_act, send, recv,
):
    dp = lax.axis_index("dp")
    s = lax.axis_index("section")
    space = lax.axis_index("space")
    y = space // 2
    last = n_sec - 1
    part = lax.rem(dp, 2)
    me = part * 2 + y
    ahead, behind = lax.rem(s + 1, n_sec), lax.rem(s + n_sec - 1, n_sec)

    def space_peer(k):
        return {"space": space ^ k}

    def plane_peer(k):
        if k == 2:
            return {"space": space ^ 2}
        return {"dp": dp ^ 1, "space": space ^ (k & 2)}

    barrier = pltpu.get_barrier_semaphore()
    partners = [space_peer(k) for k in (1, 2, 3)]
    partners += [plane_peer(k) for k in flips if k != 2]
    partners += [{"section": ahead}, {"section": behind}]
    for partner in partners:
        pl.semaphore_signal(barrier, inc=1, device_id=partner, device_id_type=MESH)

    def remote(src, dst, number, device):
        return pltpu.make_async_remote_copy(
            src_ref=src, dst_ref=dst, send_sem=send.at[number], recv_sem=recv.at[number],
            device_id=device, device_id_type=MESH,
        )

    def row_at(index):
        return pl.ds(pl.multiple_of(index * COLS, COLS), COLS)

    g_mine = g_all.at[me]
    g_cols_mine = g_cols.at[me]

    def image_row(k):
        return remote(
            images.at[(space ^ k) // 2, 0], hbuf.at[row_at(space), :], k - 1, space_peer(k)
        )

    def grad_row(k):
        return remote(
            out_grad.at[(space ^ k) // 2, 0], g_all.at[me ^ (k >> 1), row_at(space), :],
            k - 1, space_peer(k),
        )

    forward_hop = remote(obuf, hbuf, 3, {"section": ahead})
    forward_skip = remote(obuf, skip, 4, {"section": behind})
    backward_hop = remote(dbuf, g_mine, 5, {"section": behind})
    backward_skip = remote(dbuf, gskip, 6, {"section": ahead})
    act_copy = {k: remote(act_t.at[me], act_t.at[me], 6 + k, plane_peer(k)) for k in flips}
    g_copy = {k: remote(g_mine, g_mine, 9 + k, plane_peer(k)) for k in flips}
    small_copy = {k: remote(small.at[me], small.at[me], 12 + k, plane_peer(k)) for k in flips}

    angles = steps[y].astype(F32) * freqs[...]
    features = jnp.concatenate([jnp.cos(angles), jnp.sin(angles)], axis=1)
    embedded = exact_dot(jnp.broadcast_to(features, (8, C)), emb[0])[0:1]
    scales1 = 1.0 + embedded[:, :C]
    shifts = embedded[:, C:]
    gains = gain[...]
    factor = gains * scales1
    same = (
        lax.broadcasted_iota(jnp.int32, (C, C), 0) // (C // G)
        == lax.broadcasted_iota(jnp.int32, (C, C), 1) // (C // G)
    ).astype(F32).astype(BF16)
    cells = PIX * (C // G)

    clear_border(act_cols)
    for i in range(4):
        clear_border(g_cols.at[i])

    pl.semaphore_wait(barrier, len(partners))

    def turn_weights():
        for ky in range(3):
            for kx in range(3):
                turned[ky, kx * C : (kx + 1) * C, :] = weight[0, 2 - ky, 2 - kx].T

    def back_convolve():
        spread_columns(g_cols_mine, g_mine[...].astype(F32))
        d_act[...] = convolve(g_cols_mine, lambda ky: turned[ky])

    def share_grad():
        for k in flips:
            g_copy[k].start()

    @pl.when(s == 0)
    def _():
        for k in (1, 2, 3):
            image_row(k).start()
        hbuf[row_at(space), :] = images[y, 0]
        for k in (1, 2, 3):
            image_row(k).wait_recv()

    @pl.when(s == last)
    def _():
        for k in (1, 2, 3):
            grad_row(k).start()
        g_all[me, row_at(space), :] = out_grad[y, 0]
        turn_weights()
        for k in (1, 2, 3):
            grad_row(k).wait_recv()
        share_grad()
        back_convolve()

    @pl.when(s > 0)
    def _():
        forward_hop.wait_recv()

    @pl.when(s == last)
    def _():
        forward_skip.wait_recv()
        hbuf[...] = (hbuf[...].astype(F32) + skip[...].astype(F32)).astype(BF16)

    tensor = hbuf[...].astype(F32)
    first = jnp.sum(tensor, axis=0, keepdims=True)
    square = jnp.sum(tensor * tensor, axis=0, keepdims=True)
    sums = exact_dot(rows_of(first, square), same) * (1.0 / cells)
    average = sums[0:1]
    inverse = lax.rsqrt(sums[1:2] - average * average + EPS)
    normal = (tensor - average) * inverse
    normed[...] = normal
    pre = normal * factor + shifts
    sigmoid = jax.nn.sigmoid(pre)
    act = pre * sigmoid

    @pl.when(s < last)
    def _():
        spread_columns(act_cols, act)
        out = convolve(act_cols, lambda ky: weight[0, ky].reshape(3 * C, C))
        obuf[...] = (hbuf[...].astype(F32) + out).astype(BF16)
        forward_hop.start()

    @pl.when(s == 0)
    def _():
        forward_skip.start()

    slope[...] = sigmoid * (1.0 + pre * (1.0 - sigmoid))
    act_t[me] = act.astype(BF16).T
    for k in flips:
        act_copy[k].start()

    @pl.when(s < last)
    def _():
        turn_weights()
        backward_hop.wait_recv()

    @pl.when(s == 0)
    def _():
        backward_skip.wait_recv()
        g_all[me] = (g_mine[...].astype(F32) + gskip[...].astype(F32)).astype(BF16)

    @pl.when(s < last)
    def _():
        share_grad()
        back_convolve()

    d_pre = d_act[...] * slope[...]
    normal = normed[...]
    sum_pre = jnp.sum(d_pre, axis=0, keepdims=True)
    sum_normal = jnp.sum(d_pre * normal, axis=0, keepdims=True)

    @pl.when(s > 0)
    def _():
        means = exact_dot(rows_of(sum_pre * factor, sum_normal * factor), same) * (1.0 / cells)
        d_tensor = inverse * (d_pre * factor - means[0:1] - normal * means[1:2])
        dbuf[...] = (g_mine[...].astype(F32) + d_tensor).astype(BF16)
        backward_hop.start()

    @pl.when(s == last)
    def _():
        backward_skip.start()

    small[me] = rows_of(sum_normal * gains, sum_pre, sum_normal * scales1, features)
    for k in flips:
        small_copy[k].start()

    for k in flips:
        act_copy[k].wait_recv()
    for k in flips:
        g_copy[k].wait_recv()
        other = me ^ (((k & 1) << 1) | (k >> 1))
        spread_columns(g_cols.at[other], g_all[other].astype(F32))
    if len(flips) == 3:
        slots = [0, 1, 2, 3]
    else:
        slots = [part * 2, part * 2 + 1]
    for ky in range(3):
        for kx in range(3):
            total = None
            for i in slots:
                piece = jnp.dot(
                    act_t[i],
                    g_cols[i, ky * COLS : ky * COLS + PIX, kx * C : (kx + 1) * C],
                    preferred_element_type=F32,
                )
                total = piece if total is None else total + piece
            conv_out[0, 2 - ky, 2 - kx] = total

    for k in flips:
        small_copy[k].wait_recv()
    packed = [small[i] for i in slots]
    gain_total = packed[0][2:3]
    for block in packed[1:]:
        gain_total = gain_total + block[2:3]
    gain_out[...] = gain_total
    feature_rows = rows_of(*[block[3:4] for block in packed])
    d_rows = rows_of(*[jnp.concatenate([block[0:1], block[1:2]], axis=1) for block in packed])
    emb_out[0] = jnp.dot(
        feature_rows.T, d_rows, precision=lax.Precision.HIGHEST, preferred_element_type=F32
    )

    @pl.when(s == 0)
    def _():
        for k in (1, 2, 3):
            image_row(k).wait_send()
        forward_skip.wait_send()

    @pl.when(s == last)
    def _():
        for k in (1, 2, 3):
            grad_row(k).wait_send()
        backward_skip.wait_send()

    @pl.when(s < last)
    def _():
        forward_hop.wait_send()

    @pl.when(s > 0)
    def _():
        backward_hop.wait_send()

    for k in flips:
        act_copy[k].wait_send()
        g_copy[k].wait_send()
        small_copy[k].wait_send()


def per_device(images, steps, out_grad, conv_weight, gn_gain, emb_weight):
    n_dp = lax.axis_size("dp")
    n_sec = lax.axis_size("section")
    flips = (1, 2, 3) if n_dp == 2 else (2,)
    half = C // 2
    freqs = np.exp(-math.log(10000.0) * np.arange(half, dtype=np.float32) / half)
    vmem = pl.BlockSpec(memory_space=pltpu.VMEM)
    grads = pl.pallas_call(
        functools.partial(body, n_sec, flips),
        out_shape=(
            jax.ShapeDtypeStruct((1, 3, 3, C, C), F32),
            jax.ShapeDtypeStruct((1, C), F32),
            jax.ShapeDtypeStruct((1, C, 2 * C), F32),
        ),
        in_specs=[pl.BlockSpec(memory_space=pltpu.SMEM)] + [vmem] * 6,
        out_specs=(vmem, vmem, vmem),
        scratch_shapes=[
            pltpu.VMEM((PIX, C), BF16),
            pltpu.VMEM((PIX, C), BF16),
            pltpu.VMEM((PIX, C), BF16),
            pltpu.VMEM((PIX, C), BF16),
            pltpu.VMEM((PIX, C), BF16),
            pltpu.VMEM((4, C, PIX), BF16),
            pltpu.VMEM((4, PIX, C), BF16),
            pltpu.VMEM((4, 8, C), F32),
            pltpu.VMEM((3, 3 * C, C), BF16),
            pltpu.VMEM((PIX + 2 * COLS, 3 * C), BF16),
            pltpu.VMEM((4, PIX + 2 * COLS, 3 * C), BF16),
            pltpu.VMEM((PIX, C), F32),
            pltpu.VMEM((PIX, C), F32),
            pltpu.VMEM((PIX, C), F32),
            pltpu.SemaphoreType.DMA((16,)),
            pltpu.SemaphoreType.DMA((16,)),
        ],
        compiler_params=pltpu.CompilerParams(
            collective_id=0, has_side_effects=True, vmem_limit_bytes=40 * 1024 * 1024
        ),
    )(
        steps, jnp.asarray(freqs, F32)[None, :], images, out_grad, conv_weight, gn_gain, emb_weight
    )
    if n_dp != 2:
        grads = lax.psum(grads, "dp")
    return grads


def solution(mesh):
    in_specs = (
        P("dp", "space", None, None),
        P("dp"),
        P("dp", "space", None, None),
        P("section", None, None, None, None),
        P("section", None),
        P("section", None, None),
    )
    out_specs = (P("section", None, None, None, None), P("section", None), P("section", None, None))
    return jax.shard_map(
        per_device, mesh=mesh, in_specs=in_specs, out_specs=out_specs, check_vma=False
    )
```

```python
import functools
import math

import jax
import jax.numpy as jnp
import numpy as np
from jax import lax
from jax.experimental import pallas as pl
from jax.experimental.pallas import tpu as pltpu
from jax.sharding import PartitionSpec as P

G = 32
EPS = 1e-05
MESH = pl.DeviceIdType.MESH
F32 = jnp.float32
BF16 = jnp.bfloat16
PIX = 256
COLS = 64
C = 256
HALF = 128


def thirds(x):
    first = x.astype(BF16)
    rest = x - first.astype(F32)
    second = rest.astype(BF16)
    return first, second, (rest - second.astype(F32)).astype(BF16)


def exact_dot(x, matrix):
    parts = [jnp.dot(part, matrix, preferred_element_type=F32) for part in thirds(x)]
    return parts[0] + (parts[1] + parts[2])


def rows_of(*rows):
    index = lax.broadcasted_iota(jnp.int32, (8, rows[0].shape[1]), 0)
    out = jnp.zeros((8, rows[0].shape[1]), F32)
    for i, row in enumerate(rows):
        out = jnp.where(index == i, row, out)
    return out


def half_at(index):
    return pl.ds(pl.multiple_of(index * HALF, HALF), HALF)


def spread_columns(ref, value, half):
    column = lax.broadcasted_iota(jnp.int32, (PIX, HALF), 0) & (COLS - 1)
    left = jnp.where(column == 0, 0.0, pltpu.roll(value, 1, 0))
    right = jnp.where(column == COLS - 1, 0.0, pltpu.roll(value, PIX - 1, 0))
    for kx, moved in enumerate((left, value, right)):
        ref[COLS : COLS + PIX, half_at(2 * kx + half)] = moved.astype(BF16)


def clear_border(ref):
    blank = jnp.zeros((COLS, 3 * C), BF16)
    ref[0:COLS, :] = blank
    ref[COLS + PIX : 2 * COLS + PIX, :] = blank


def convolve(ref, kernel, half):
    total = None
    for ky in range(3):
        rows = slice(ky * COLS, ky * COLS + PIX)
        left = jnp.concatenate([ref[rows, half_at(2 * kx + half)] for kx in range(3)], axis=1)
        right = kernel[ky, :, half_at(half), :].reshape(3 * HALF, HALF)
        part = jnp.dot(left, right, preferred_element_type=F32)
        total = part if total is None else total + part
    return total


def chain_body(
    n_sec, flips, steps, freqs, images, out_grad, weight, gain, emb,
    act_out, cols_out, small_out,
    act_t, g_cols, small, hbuf, skip, gskip, obuf, dbuf, act_raw, g_all, plain, across, turned, act_cols,
    normed, slope, d_act, freqs_v, gain_v, emb_v, send, recv, local, leave,
):
    dp = lax.axis_index("dp")
    s = lax.axis_index("section")
    space = lax.axis_index("space")
    y = space // 2
    core = lax.rem(space, 2)
    last = n_sec - 1
    me = dp * 2 + y if len(flips) == 3 else y
    ahead, behind = lax.rem(s + 1, n_sec), lax.rem(s + n_sec - 1, n_sec)
    sibling = {"space": space ^ 1}

    def plane_peer(k, flip_core=0):
        return {"dp": dp ^ (k & 1), "space": space ^ (k & 2) ^ flip_core}

    others = [(k, f) for k in (0,) + flips for f in (0, 1) if k or f]
    barrier = pltpu.get_barrier_semaphore()
    partners = [plane_peer(k, f) if k & 1 else {"space": space ^ (k & 2) ^ f} for k, f in others]
    partners += [{"section": ahead}, {"section": behind}]
    for partner in partners:
        pl.semaphore_signal(barrier, inc=1, device_id=partner, device_id_type=MESH)

    loads = [
        pltpu.make_async_copy(src, dst, local.at[i])
        for i, (src, dst) in enumerate((
            (freqs, freqs_v),
            (emb.at[0, :, half_at(core)], emb_v.at[0]),
            (emb.at[0, :, half_at(core + 2)], emb_v.at[1]),
            (gain.at[:, half_at(core)], gain_v),
            (weight.at[0, :, :, :, half_at(core)], plain),
            (weight.at[0, :, :, half_at(core), :], across),
        ))
    ]
    for load in loads:
        load.start()

    def remote(src, dst, number, device):
        return pltpu.make_async_remote_copy(
            src_ref=src, dst_ref=dst, send_sem=send.at[number], recv_sem=recv.at[number],
            device_id=device, device_id_type=MESH,
        )

    def row_at(index):
        return pl.ds(pl.multiple_of(index * COLS, COLS), COLS)

    g_mine = g_all.at[me, core]
    g_cols_mine = g_cols.at[me]
    act_rows = half_at(core)

    def image_row(k):
        target = space ^ k
        return remote(
            images.at[target // 2, 0, :, half_at(lax.rem(target, 2))],
            hbuf.at[row_at(space), :], k - 1, {"space": target},
        )

    def grad_row(k):
        target = space ^ k
        return remote(
            out_grad.at[target // 2, 0, :, half_at(lax.rem(target, 2))],
            g_all.at[me ^ (k >> 1), lax.rem(target, 2), row_at(space), :],
            k - 1, {"space": target},
        )

    own_image = pltpu.make_async_copy(
        images.at[y, 0, :, half_at(core)], hbuf.at[row_at(space), :], local.at[6]
    )
    own_grad = pltpu.make_async_copy(
        out_grad.at[y, 0, :, half_at(core)], g_all.at[me, core, row_at(space), :], local.at[6]
    )
    forward_hop = remote(obuf, hbuf, 3, {"section": ahead})
    forward_skip = remote(obuf, skip, 4, {"section": behind})
    backward_hop = remote(dbuf, g_mine, 5, {"section": behind})
    backward_skip = remote(dbuf, gskip, 6, {"section": ahead})
    act_sibling = remote(act_raw.at[core], act_raw.at[core], 7, sibling)
    g_sibling = remote(g_mine, g_mine, 8, sibling)
    act_copy, g_copy, act_pass, g_pass, slot = {}, {}, {}, {}, {}
    for k in flips:
        slot[k] = me ^ (((k & 1) << 1) | (k >> 1))
        mine = act_t.at[me, act_rows, :]
        theirs = act_t.at[slot[k], act_rows, :]
        act_copy[k] = remote(mine, mine, 8 + k, plane_peer(k))
        g_copy[k] = remote(g_mine, g_mine, 11 + k, plane_peer(k))
        act_pass[k] = remote(theirs, theirs, 14 + k, sibling)
        passed = g_all.at[slot[k], core]
        g_pass[k] = remote(passed, passed, 17 + k, sibling)
    small_copy = [
        remote(small.at[me, core], small.at[me, core], 21 + i, plane_peer(k, f))
        for i, (k, f) in enumerate(others)
    ]

    clear_border(act_cols)
    for i in range(4):
        clear_border(g_cols.at[i])
    same = (
        lax.broadcasted_iota(jnp.int32, (HALF, HALF), 0) // (C // G)
        == lax.broadcasted_iota(jnp.int32, (HALF, HALF), 1) // (C // G)
    ).astype(F32).astype(BF16)
    cells = PIX * (C // G)

    pl.semaphore_wait(barrier, len(partners))

    @pl.when(s == 0)
    def _():
        for k in (1, 2, 3):
            image_row(k).start()
        own_image.start()

    @pl.when(s == last)
    def _():
        for k in (1, 2, 3):
            grad_row(k).start()
        own_grad.start()

    for load in loads[:4]:
        load.wait()
    angles = steps[y].astype(F32) * freqs_v[...]
    cosines, sines = jnp.cos(angles), jnp.sin(angles)
    features = jnp.broadcast_to(jnp.concatenate([cosines, sines], axis=1), (8, C))
    scales1 = 1.0 + exact_dot(features, emb_v[0])[0:1]
    shifts = exact_dot(features, emb_v[1])[0:1]
    gains = gain_v[...]
    factor = gains * scales1
    for load in loads[4:]:
        load.wait()

    def turn_weights():
        for ky in range(3):
            for kx in range(3):
                turned[ky, kx] = across[2 - ky, 2 - kx].T

    def back_convolve():
        g_sibling.start()
        for k in flips:
            g_copy[k].start()
        spread_columns(g_cols_mine, g_mine[...].astype(F32), core)
        total = convolve(g_cols_mine, turned, core)
        g_sibling.wait_recv()
        spread_columns(g_cols_mine, g_all[me, 1 - core].astype(F32), 1 - core)
        d_act[...] = total + convolve(g_cols_mine, turned, 1 - core)

    @pl.when(s == 0)
    def _():
        own_image.wait()
        for k in (1, 2, 3):
            image_row(k).wait_recv()

    @pl.when(s == last)
    def _():
        turn_weights()
        own_grad.wait()
        for k in (1, 2, 3):
            grad_row(k).wait_recv()
        back_convolve()

    @pl.when(s > 0)
    def _():
        forward_hop.wait_recv()

    @pl.when(s == last)
    def _():
        forward_skip.wait_recv()
        hbuf[...] = (hbuf[...].astype(F32) + skip[...].astype(F32)).astype(BF16)

    tensor = hbuf[...].astype(F32)
    first = jnp.sum(tensor, axis=0, keepdims=True)
    square = jnp.sum(tensor * tensor, axis=0, keepdims=True)
    sums = exact_dot(rows_of(first, square), same) * (1.0 / cells)
    average = sums[0:1]
    inverse = lax.rsqrt(sums[1:2] - average * average + EPS)
    normal = (tensor - average) * inverse
    normed[...] = normal
    pre = normal * factor + shifts
    sigmoid = jax.nn.sigmoid(pre)
    act = pre * sigmoid
    act_raw[core] = act.astype(BF16)
    act_sibling.start()

    @pl.when(s < last)
    def _():
        spread_columns(act_cols, act, core)
        out = hbuf[...].astype(F32) + convolve(act_cols, plain, core)
        act_sibling.wait_recv()
        spread_columns(act_cols, act_raw[1 - core].astype(F32), 1 - core)
        obuf[...] = (out + convolve(act_cols, plain, 1 - core)).astype(BF16)
        forward_hop.start()

    @pl.when(s == 0)
    def _():
        forward_skip.start()

    slope[...] = sigmoid * (1.0 + pre * (1.0 - sigmoid))

    def share_act():
        act_t[me, act_rows, :] = act_raw[core].T
        for k in flips:
            act_copy[k].start()
        act_t[me, half_at(1 - core), :] = act_raw[1 - core].T

    @pl.when(s < last)
    def _():
        share_act()
        turn_weights()
        backward_hop.wait_recv()

    @pl.when(s == 0)
    def _():
        backward_skip.wait_recv()
        g_all[me, core] = (g_mine[...].astype(F32) + gskip[...].astype(F32)).astype(BF16)

    @pl.when(s < last)
    def _():
        back_convolve()

    d_pre = d_act[...] * slope[...]
    normal = normed[...]
    sum_pre = jnp.sum(d_pre, axis=0, keepdims=True)
    sum_normal = jnp.sum(d_pre * normal, axis=0, keepdims=True)

    @pl.when(s > 0)
    def _():
        means = exact_dot(rows_of(sum_pre * factor, sum_normal * factor), same) * (1.0 / cells)
        d_tensor = inverse * (d_pre * factor - means[0:1] - normal * means[1:2])
        dbuf[...] = (g_mine[...].astype(F32) + d_tensor).astype(BF16)
        backward_hop.start()

    @pl.when(s == last)
    def _():
        backward_skip.start()
        act_sibling.wait_recv()
        share_act()

    small[me, core] = rows_of(sum_normal * gains, sum_pre, sum_normal * scales1, cosines, sines)
    for copy in small_copy:
        copy.start()

    def image_out(slot_no, number):
        return [
            pltpu.make_async_copy(act_t.at[slot_no], act_out.at[slot_no], leave.at[number]),
            pltpu.make_async_copy(g_cols.at[slot_no], cols_out.at[slot_no], leave.at[4 + number]),
        ]

    leaving = image_out(me, 0)
    for copy in leaving:
        copy.start()

    for k in flips:
        act_copy[k].wait_recv()
        act_pass[k].start()
    for k in flips:
        g_copy[k].wait_recv()
        g_pass[k].start()
        spread_columns(g_cols.at[slot[k]], g_all[slot[k], core].astype(F32), core)
    for k in flips:
        act_pass[k].wait_recv()
        g_pass[k].wait_recv()
        spread_columns(g_cols.at[slot[k]], g_all[slot[k], 1 - core].astype(F32), 1 - core)
        for copy in image_out(slot[k], k):
            copy.start()
            leaving.append(copy)
    for copy in small_copy:
        copy.wait_recv()
    leaving.append(pltpu.make_async_copy(small, small_out, leave.at[8]))
    leaving[-1].start()

    @pl.when(s == 0)
    def _():
        for k in (1, 2, 3):
            image_row(k).wait_send()
        forward_skip.wait_send()

    @pl.when(s == last)
    def _():
        for k in (1, 2, 3):
            grad_row(k).wait_send()
        backward_skip.wait_send()

    @pl.when(s < last)
    def _():
        forward_hop.wait_send()

    @pl.when(s > 0)
    def _():
        backward_hop.wait_send()

    act_sibling.wait_send()
    g_sibling.wait_send()
    for k in flips:
        for copy in (act_copy[k], g_copy[k], act_pass[k], g_pass[k]):
            copy.wait_send()
    for copy in small_copy:
        copy.wait_send()
    for copy in leaving:
        copy.wait()


def grad_body(
    slots, act_in, cols_in, small_in, conv_out, gain_out, emb_out,
    act_t, g_cols, small, taps, gain_v, emb_v, sems,
):
    loads = [pltpu.make_async_copy(small_in, small, sems.at[11])]
    for i in range(slots):
        loads.append(pltpu.make_async_copy(act_in.at[i], act_t.at[i], sems.at[12 + i]))
        loads.append(pltpu.make_async_copy(cols_in.at[i], g_cols.at[i], sems.at[16 + i]))
    for load in loads:
        load.start()
    loads[0].wait()
    packed = [jnp.concatenate([small[i, 0], small[i, 1]], axis=1) for i in range(slots)]
    gain_total = packed[0][2:3]
    for block in packed[1:]:
        gain_total = gain_total + block[2:3]
    gain_v[...] = gain_total
    features = rows_of(
        *[jnp.concatenate([small[i, 0, 3:4], small[i, 0, 4:5]], axis=1) for i in range(slots)]
    )
    d_rows = rows_of(*[jnp.concatenate([block[0:1], block[1:2]], axis=1) for block in packed])
    emb_v[...] = jnp.dot(
        features.T, d_rows, precision=lax.Precision.HIGHEST, preferred_element_type=F32
    )
    copies = [
        pltpu.make_async_copy(gain_v, gain_out, sems.at[9]),
        pltpu.make_async_copy(emb_v, emb_out.at[0], sems.at[10]),
    ]
    for copy in copies:
        copy.start()
    for load in loads[1:]:
        load.wait()
    for ky in range(3):
        for kx in range(3):
            total = None
            for i in range(slots):
                piece = jnp.dot(
                    act_t[i],
                    g_cols[i, ky * COLS : ky * COLS + PIX, kx * C : (kx + 1) * C],
                    preferred_element_type=F32,
                )
                total = piece if total is None else total + piece
            tap = ky * 3 + kx
            taps[tap] = total
            copy = pltpu.make_async_copy(taps.at[tap], conv_out.at[0, 2 - ky, 2 - kx], sems.at[tap])
            copy.start()
            copies.append(copy)
    for copy in copies:
        copy.wait()


def per_device(images, steps, out_grad, conv_weight, gn_gain, emb_weight):
    n_dp = lax.axis_size("dp")
    n_sec = lax.axis_size("section")
    flips = (1, 2, 3) if n_dp == 2 else (2,)
    half = C // 2
    freqs = np.exp(-math.log(10000.0) * np.arange(half, dtype=np.float32) / half)
    hbm = pl.BlockSpec(memory_space=pltpu.HBM)
    padded = PIX + 2 * COLS
    chain = pl.pallas_call(
        functools.partial(chain_body, n_sec, flips),
        out_shape=(
            jax.ShapeDtypeStruct((4, C, PIX), BF16),
            jax.ShapeDtypeStruct((4, padded, 3 * C), BF16),
            jax.ShapeDtypeStruct((4, 2, 8, HALF), F32),
        ),
        in_specs=[pl.BlockSpec(memory_space=pltpu.SMEM)] + [hbm] * 6,
        out_specs=(hbm, hbm, hbm),
        scratch_shapes=[
            pltpu.VMEM((4, C, PIX), BF16),
            pltpu.VMEM((4, padded, 3 * C), BF16),
            pltpu.VMEM((4, 2, 8, HALF), F32),
            pltpu.VMEM((PIX, HALF), BF16),
            pltpu.VMEM((PIX, HALF), BF16),
            pltpu.VMEM((PIX, HALF), BF16),
            pltpu.VMEM((PIX, HALF), BF16),
            pltpu.VMEM((PIX, HALF), BF16),
            pltpu.VMEM((2, PIX, HALF), BF16),
            pltpu.VMEM((4, 2, PIX, HALF), BF16),
            pltpu.VMEM((3, 3, C, HALF), BF16),
            pltpu.VMEM((3, 3, HALF, C), BF16),
            pltpu.VMEM((3, 3, C, HALF), BF16),
            pltpu.VMEM((padded, 3 * C), BF16),
            pltpu.VMEM((PIX, HALF), F32),
            pltpu.VMEM((PIX, HALF), F32),
            pltpu.VMEM((PIX, HALF), F32),
            pltpu.VMEM((1, HALF), F32),
            pltpu.VMEM((1, HALF), F32),
            pltpu.VMEM((2, C, HALF), BF16),
            pltpu.SemaphoreType.DMA((28,)),
            pltpu.SemaphoreType.DMA((28,)),
            pltpu.SemaphoreType.DMA((7,)),
            pltpu.SemaphoreType.DMA((9,)),
        ],
        compiler_params=pltpu.CompilerParams(
            collective_id=0, has_side_effects=True, vmem_limit_bytes=56 * 1024 * 1024
        ),
    )(
        steps, jnp.asarray(freqs, F32)[None, :], images, out_grad, conv_weight, gn_gain, emb_weight
    )
    grads = pl.pallas_call(
        functools.partial(grad_body, 4 if n_dp == 2 else 2),
        out_shape=(
            jax.ShapeDtypeStruct((1, 3, 3, C, C), F32),
            jax.ShapeDtypeStruct((1, C), F32),
            jax.ShapeDtypeStruct((1, C, 2 * C), F32),
        ),
        in_specs=[hbm] * 3,
        out_specs=(hbm, hbm, hbm),
        scratch_shapes=[
            pltpu.VMEM((4, C, PIX), BF16),
            pltpu.VMEM((4, padded, 3 * C), BF16),
            pltpu.VMEM((4, 2, 8, HALF), F32),
            pltpu.VMEM((9, C, C), F32),
            pltpu.VMEM((1, C), F32),
            pltpu.VMEM((C, 2 * C), F32),
            pltpu.SemaphoreType.DMA((20,)),
        ],
        compiler_params=pltpu.CompilerParams(vmem_limit_bytes=56 * 1024 * 1024),
    )(*chain)
    if n_dp != 2:
        grads = lax.psum(grads, "dp")
    return grads


def solution(mesh):
    in_specs = (
        P("dp", "space", None, None),
        P("dp"),
        P("dp", "space", None, None),
        P("section", None, None, None, None),
        P("section", None),
        P("section", None, None),
    )
    out_specs = (P("section", None, None, None, None), P("section", None), P("section", None, None))
    return jax.shard_map(
        per_device, mesh=mesh, in_specs=in_specs, out_specs=out_specs, check_vma=False
    )
```

```python
import functools
import math

import jax
import jax.numpy as jnp
import numpy as np
from jax import lax
from jax.experimental import pallas as pl
from jax.experimental.pallas import tpu as pltpu
from jax.sharding import PartitionSpec as P

G = 32
EPS = 1e-05
MESH = pl.DeviceIdType.MESH
F32 = jnp.float32
BF16 = jnp.bfloat16
PIX = 256
COLS = 64
C = 256
HALF = 128


def thirds(x):
    first = x.astype(BF16)
    rest = x - first.astype(F32)
    second = rest.astype(BF16)
    return first, second, (rest - second.astype(F32)).astype(BF16)


def exact_dot(x, matrix):
    parts = [jnp.dot(part, matrix, preferred_element_type=F32) for part in thirds(x)]
    return parts[0] + (parts[1] + parts[2])


def rows_of(*rows):
    index = lax.broadcasted_iota(jnp.int32, (8, rows[0].shape[1]), 0)
    out = jnp.zeros((8, rows[0].shape[1]), F32)
    for i, row in enumerate(rows):
        out = jnp.where(index == i, row, out)
    return out


def half_at(index):
    return pl.ds(pl.multiple_of(index * HALF, HALF), HALF)


def group_means(first, second, same, scale):
    parts = [p.astype(F32) for p in thirds(first) + thirds(second)]
    sums = jnp.dot(rows_of(*parts).astype(BF16), same, preferred_element_type=F32) * scale
    return sums[0:1] + (sums[1:2] + sums[2:3]), sums[3:4] + (sums[4:5] + sums[5:6])


def spread_columns(ref, value, half):
    column = lax.broadcasted_iota(jnp.int32, (PIX, HALF), 0) & (COLS - 1)
    left = jnp.where(column == 0, 0.0, pltpu.roll(value, 1, 0))
    right = jnp.where(column == COLS - 1, 0.0, pltpu.roll(value, PIX - 1, 0))
    for kx, moved in enumerate((left, value, right)):
        ref[COLS : COLS + PIX, half_at(2 * kx + half)] = moved.astype(BF16)


def clear_border(ref):
    blank = jnp.zeros((COLS, 3 * C), BF16)
    ref[0:COLS, :] = blank
    ref[COLS + PIX : 2 * COLS + PIX, :] = blank


def convolve(ref, kernel, half, start=0, count=PIX):
    left = jnp.concatenate(
        [
            ref[ky * COLS + start : ky * COLS + start + count, half_at(2 * kx + half)]
            for ky in range(3)
            for kx in range(3)
        ],
        axis=1,
    )
    right = kernel[:, :, half_at(half), :].reshape(9 * HALF, HALF)
    return jnp.dot(left, right, preferred_element_type=F32)


def chain_body(
    n_sec, flips, steps, freqs, images, out_grad, weight, gain, emb,
    act_out, cols_out, small_out,
    act_t, g_cols, small, hbuf, skip, gskip, obuf, dbuf, act_raw, g_all, plain, across, turned, act_cols,
    normed, slope, d_act, freqs_v, gain_v, emb_v, send, recv, local, leave,
):
    dp = lax.axis_index("dp")
    s = lax.axis_index("section")
    space = lax.axis_index("space")
    y = space // 2
    core = lax.rem(space, 2)
    last = n_sec - 1
    me = dp * 2 + y if len(flips) == 3 else y
    ahead, behind = lax.rem(s + 1, n_sec), lax.rem(s + n_sec - 1, n_sec)
    sibling = {"space": space ^ 1}

    def plane_peer(k, flip_core=0):
        return {"dp": dp ^ (k & 1), "space": space ^ (k & 2) ^ flip_core}

    others = [(k, f) for k in (0,) + flips for f in (0, 1) if k or f]
    barrier = pltpu.get_barrier_semaphore()
    partners = [plane_peer(k, f) if k & 1 else {"space": space ^ (k & 2) ^ f} for k, f in others]
    partners += [{"section": ahead}, {"section": behind}]
    for partner in partners:
        pl.semaphore_signal(barrier, inc=1, device_id=partner, device_id_type=MESH)

    loads = [
        pltpu.make_async_copy(src, dst, local.at[i])
        for i, (src, dst) in enumerate((
            (freqs, freqs_v),
            (emb.at[0, :, half_at(core)], emb_v.at[0]),
            (emb.at[0, :, half_at(core + 2)], emb_v.at[1]),
            (gain.at[:, half_at(core)], gain_v),
            (weight.at[0, :, :, :, half_at(core)], plain),
            (weight.at[0, :, :, half_at(core), :], across),
        ))
    ]
    for load in loads:
        load.start()

    def remote(src, dst, number, device):
        return pltpu.make_async_remote_copy(
            src_ref=src, dst_ref=dst, send_sem=send.at[number], recv_sem=recv.at[number],
            device_id=device, device_id_type=MESH,
        )

    def row_at(index):
        return pl.ds(pl.multiple_of(index * COLS, COLS), COLS)

    g_mine = g_all.at[me, core]
    g_cols_mine = g_cols.at[me]
    act_rows = half_at(core)

    def image_row(k):
        target = space ^ k
        return remote(
            images.at[target // 2, 0, :, half_at(lax.rem(target, 2))],
            hbuf.at[row_at(space), :], k - 1, {"space": target},
        )

    def grad_row(k):
        target = space ^ k
        return remote(
            out_grad.at[target // 2, 0, :, half_at(lax.rem(target, 2))],
            g_all.at[me ^ (k >> 1), lax.rem(target, 2), row_at(space), :],
            k - 1, {"space": target},
        )

    own_image = pltpu.make_async_copy(
        images.at[y, 0, :, half_at(core)], hbuf.at[row_at(space), :], local.at[6]
    )
    own_grad = pltpu.make_async_copy(
        out_grad.at[y, 0, :, half_at(core)], g_all.at[me, core, row_at(space), :], local.at[6]
    )
    pieces = [slice(0, PIX // 2), slice(PIX // 2, PIX)]
    forward_hop = [
        remote(obuf.at[piece, :], hbuf.at[piece, :], number, {"section": ahead})
        for piece, number in zip(pieces, (3, 28))
    ]
    forward_skip = remote(obuf, skip, 4, {"section": behind})
    backward_hop = remote(dbuf, g_mine, 5, {"section": behind})
    backward_skip = remote(dbuf, gskip, 6, {"section": ahead})
    act_sibling = remote(act_raw.at[core], act_raw.at[core], 7, sibling)
    g_sibling = remote(g_mine, g_mine, 8, sibling)
    act_copy, g_copy, act_pass, g_pass, slot = {}, {}, {}, {}, {}
    for k in flips:
        slot[k] = me ^ (((k & 1) << 1) | (k >> 1))
        mine = act_t.at[me, act_rows, :]
        theirs = act_t.at[slot[k], act_rows, :]
        act_copy[k] = remote(mine, mine, 8 + k, plane_peer(k))
        g_copy[k] = remote(g_mine, g_mine, 11 + k, plane_peer(k))
        act_pass[k] = remote(theirs, theirs, 14 + k, sibling)
        passed = g_all.at[slot[k], core]
        g_pass[k] = remote(passed, passed, 17 + k, sibling)
    small_copy = [
        remote(small.at[me, core], small.at[me, core], 21 + i, plane_peer(k, f))
        for i, (k, f) in enumerate(others)
    ]

    clear_border(act_cols)
    for i in range(4):
        clear_border(g_cols.at[i])
    same = (
        lax.broadcasted_iota(jnp.int32, (HALF, HALF), 0) // (C // G)
        == lax.broadcasted_iota(jnp.int32, (HALF, HALF), 1) // (C // G)
    ).astype(F32).astype(BF16)
    cells = PIX * (C // G)

    pl.semaphore_wait(barrier, len(partners))

    @pl.when(s == 0)
    def _():
        for k in (1, 2, 3):
            image_row(k).start()
        own_image.start()

    @pl.when(s == last)
    def _():
        for k in (1, 2, 3):
            grad_row(k).start()
        own_grad.start()

    for load in loads[:4]:
        load.wait()
    angles = steps[y].astype(F32) * freqs_v[...]
    cosines, sines = jnp.cos(angles), jnp.sin(angles)
    features = jnp.broadcast_to(jnp.concatenate([cosines, sines], axis=1), (8, C))
    scales1 = 1.0 + exact_dot(features, emb_v[0])[0:1]
    shifts = exact_dot(features, emb_v[1])[0:1]
    gains = gain_v[...]
    factor = gains * scales1
    for load in loads[4:]:
        load.wait()

    def turn_weights():
        for ky in range(3):
            for kx in range(3):
                turned[ky, kx] = across[2 - ky, 2 - kx].T

    def back_convolve():
        g_sibling.start()
        spread_columns(g_cols_mine, g_mine[...].astype(F32), core)
        total = convolve(g_cols_mine, turned, core)
        g_sibling.wait_recv()
        spread_columns(g_cols_mine, g_all[me, 1 - core].astype(F32), 1 - core)
        d_act[...] = total + convolve(g_cols_mine, turned, 1 - core)

    @pl.when(s == 0)
    def _():
        own_image.wait()
        for k in (1, 2, 3):
            image_row(k).wait_recv()

    @pl.when(s == last)
    def _():
        turn_weights()
        own_grad.wait()
        for k in (1, 2, 3):
            grad_row(k).wait_recv()
        back_convolve()

    @pl.when(s > 0)
    def _():
        for hop in forward_hop:
            hop.wait_recv()

    @pl.when(s == last)
    def _():
        forward_skip.wait_recv()
        hbuf[...] = (hbuf[...].astype(F32) + skip[...].astype(F32)).astype(BF16)

    tensor = hbuf[...].astype(F32)
    first = jnp.sum(tensor, axis=0, keepdims=True)
    square = jnp.sum(tensor * tensor, axis=0, keepdims=True)
    average, mean_square = group_means(first, square, same, 1.0 / cells)
    inverse = lax.rsqrt(mean_square - average * average + EPS)
    normal = (tensor - average) * inverse
    normed[...] = normal
    pre = normal * factor + shifts
    sigmoid = jax.nn.sigmoid(pre)
    act = pre * sigmoid
    act_raw[core] = act.astype(BF16)
    act_sibling.start()

    @pl.when(s < last)
    def _():
        spread_columns(act_cols, act, core)
        out = hbuf[...].astype(F32) + convolve(act_cols, plain, core)
        act_sibling.wait_recv()
        spread_columns(act_cols, act_raw[1 - core].astype(F32), 1 - core)
        for piece, hop in zip(pieces, forward_hop):
            more = convolve(act_cols, plain, 1 - core, piece.start, PIX // 2)
            obuf[piece, :] = (out[piece] + more).astype(BF16)
            hop.start()

    @pl.when(s == 0)
    def _():
        forward_skip.start()

    slope[...] = sigmoid * (1.0 + pre * (1.0 - sigmoid))

    def share_act():
        act_t[me, act_rows, :] = act_raw[core].T
        for k in flips:
            act_copy[k].start()
        act_t[me, half_at(1 - core), :] = act_raw[1 - core].T

    @pl.when(s < last)
    def _():
        share_act()
        turn_weights()
        backward_hop.wait_recv()

    @pl.when(s == 0)
    def _():
        backward_skip.wait_recv()
        g_all[me, core] = (g_mine[...].astype(F32) + gskip[...].astype(F32)).astype(BF16)

    def share_grad():
        for k in reversed(flips):
            g_copy[k].start()

    @pl.when(s == 0)
    def _():
        share_grad()

    @pl.when(s < last)
    def _():
        back_convolve()

    d_pre = d_act[...] * slope[...]
    normal = normed[...]
    sum_pre = jnp.sum(d_pre, axis=0, keepdims=True)
    sum_normal = jnp.sum(d_pre * normal, axis=0, keepdims=True)

    @pl.when(s > 0)
    def _():
        mean_d, mean_dn = group_means(sum_pre * factor, sum_normal * factor, same, 1.0 / cells)
        d_tensor = inverse * (d_pre * factor - mean_d - normal * mean_dn)
        dbuf[...] = (g_mine[...].astype(F32) + d_tensor).astype(BF16)
        backward_hop.start()
        share_grad()

    @pl.when(s == last)
    def _():
        backward_skip.start()
        act_sibling.wait_recv()
        share_act()

    small[me, core] = rows_of(sum_normal * gains, sum_pre, sum_normal * scales1, cosines, sines)
    for copy in small_copy:
        copy.start()

    def image_out(slot_no, number):
        return [
            pltpu.make_async_copy(act_t.at[slot_no], act_out.at[slot_no], leave.at[number]),
            pltpu.make_async_copy(g_cols.at[slot_no], cols_out.at[slot_no], leave.at[4 + number]),
        ]

    leaving = image_out(me, 0)
    for copy in leaving:
        copy.start()

    for k in flips:
        act_copy[k].wait_recv()
        act_pass[k].start()
    for k in flips:
        g_copy[k].wait_recv()
        g_pass[k].start()
        spread_columns(g_cols.at[slot[k]], g_all[slot[k], core].astype(F32), core)
    for k in flips:
        act_pass[k].wait_recv()
        g_pass[k].wait_recv()
        spread_columns(g_cols.at[slot[k]], g_all[slot[k], 1 - core].astype(F32), 1 - core)
        for copy in image_out(slot[k], k):
            copy.start()
            leaving.append(copy)
    for copy in small_copy:
        copy.wait_recv()
    leaving.append(pltpu.make_async_copy(small, small_out, leave.at[8]))
    leaving[-1].start()

    @pl.when(s == 0)
    def _():
        for k in (1, 2, 3):
            image_row(k).wait_send()
        forward_skip.wait_send()

    @pl.when(s == last)
    def _():
        for k in (1, 2, 3):
            grad_row(k).wait_send()
        backward_skip.wait_send()

    @pl.when(s < last)
    def _():
        for hop in forward_hop:
            hop.wait_send()

    @pl.when(s > 0)
    def _():
        backward_hop.wait_send()

    act_sibling.wait_send()
    g_sibling.wait_send()
    for k in flips:
        for copy in (act_copy[k], g_copy[k], act_pass[k], g_pass[k]):
            copy.wait_send()
    for copy in small_copy:
        copy.wait_send()
    for copy in leaving:
        copy.wait()


def grad_body(
    slots, act_in, cols_in, small_in, conv_out, gain_out, emb_out,
    act_t, g_cols, small, taps, gain_v, emb_v, sems,
):
    loads = [pltpu.make_async_copy(small_in, small, sems.at[11])]
    for i in range(slots):
        loads.append(pltpu.make_async_copy(act_in.at[i], act_t.at[i], sems.at[12 + i]))
    shifted = []
    for kx in range(3):
        lanes = slice(kx * C, (kx + 1) * C)
        shifted.append([
            pltpu.make_async_copy(
                cols_in.at[i, :, lanes], g_cols.at[i, :, lanes], sems.at[16 + 4 * kx + i]
            )
            for i in range(slots)
        ])
    for load in loads + shifted[0] + shifted[1] + shifted[2]:
        load.start()
    loads[0].wait()
    packed = [jnp.concatenate([small[i, 0], small[i, 1]], axis=1) for i in range(slots)]
    gain_total = packed[0][2:3]
    for block in packed[1:]:
        gain_total = gain_total + block[2:3]
    gain_v[...] = gain_total
    features = rows_of(
        *[jnp.concatenate([small[i, 0, 3:4], small[i, 0, 4:5]], axis=1) for i in range(slots)]
    )
    d_rows = rows_of(*[jnp.concatenate([block[0:1], block[1:2]], axis=1) for block in packed])
    emb_v[...] = jnp.dot(
        features.T, d_rows, precision=lax.Precision.HIGHEST, preferred_element_type=F32
    )
    copies = [
        pltpu.make_async_copy(gain_v, gain_out, sems.at[9]),
        pltpu.make_async_copy(emb_v, emb_out.at[0], sems.at[10]),
    ]
    for copy in copies:
        copy.start()
    for load in loads[1:]:
        load.wait()
    for kx in range(3):
        for load in shifted[kx]:
            load.wait()
        for ky in range(3):
            total = None
            for i in range(slots):
                piece = jnp.dot(
                    act_t[i],
                    g_cols[i, ky * COLS : ky * COLS + PIX, kx * C : (kx + 1) * C],
                    preferred_element_type=F32,
                )
                total = piece if total is None else total + piece
            tap = ky * 3 + kx
            taps[tap] = total
            copy = pltpu.make_async_copy(taps.at[tap], conv_out.at[0, 2 - ky, 2 - kx], sems.at[tap])
            copy.start()
            copies.append(copy)
    for copy in copies:
        copy.wait()


def per_device(images, steps, out_grad, conv_weight, gn_gain, emb_weight):
    n_dp = lax.axis_size("dp")
    n_sec = lax.axis_size("section")
    flips = (1, 2, 3) if n_dp == 2 else (2,)
    half = C // 2
    freqs = np.exp(-math.log(10000.0) * np.arange(half, dtype=np.float32) / half)
    hbm = pl.BlockSpec(memory_space=pltpu.HBM)
    padded = PIX + 2 * COLS
    chain = pl.pallas_call(
        functools.partial(chain_body, n_sec, flips),
        out_shape=(
            jax.ShapeDtypeStruct((4, C, PIX), BF16),
            jax.ShapeDtypeStruct((4, padded, 3 * C), BF16),
            jax.ShapeDtypeStruct((4, 2, 8, HALF), F32),
        ),
        in_specs=[pl.BlockSpec(memory_space=pltpu.SMEM)] + [hbm] * 6,
        out_specs=(hbm, hbm, hbm),
        scratch_shapes=[
            pltpu.VMEM((4, C, PIX), BF16),
            pltpu.VMEM((4, padded, 3 * C), BF16),
            pltpu.VMEM((4, 2, 8, HALF), F32),
            pltpu.VMEM((PIX, HALF), BF16),
            pltpu.VMEM((PIX, HALF), BF16),
            pltpu.VMEM((PIX, HALF), BF16),
            pltpu.VMEM((PIX, HALF), BF16),
            pltpu.VMEM((PIX, HALF), BF16),
            pltpu.VMEM((2, PIX, HALF), BF16),
            pltpu.VMEM((4, 2, PIX, HALF), BF16),
            pltpu.VMEM((3, 3, C, HALF), BF16),
            pltpu.VMEM((3, 3, HALF, C), BF16),
            pltpu.VMEM((3, 3, C, HALF), BF16),
            pltpu.VMEM((padded, 3 * C), BF16),
            pltpu.VMEM((PIX, HALF), F32),
            pltpu.VMEM((PIX, HALF), F32),
            pltpu.VMEM((PIX, HALF), F32),
            pltpu.VMEM((1, HALF), F32),
            pltpu.VMEM((1, HALF), F32),
            pltpu.VMEM((2, C, HALF), BF16),
            pltpu.SemaphoreType.DMA((29,)),
            pltpu.SemaphoreType.DMA((29,)),
            pltpu.SemaphoreType.DMA((7,)),
            pltpu.SemaphoreType.DMA((9,)),
        ],
        compiler_params=pltpu.CompilerParams(
            collective_id=0, has_side_effects=True, vmem_limit_bytes=56 * 1024 * 1024
        ),
    )(
        steps, jnp.asarray(freqs, F32)[None, :], images, out_grad, conv_weight, gn_gain, emb_weight
    )
    grads = pl.pallas_call(
        functools.partial(grad_body, 4 if n_dp == 2 else 2),
        out_shape=(
            jax.ShapeDtypeStruct((1, 3, 3, C, C), F32),
            jax.ShapeDtypeStruct((1, C), F32),
            jax.ShapeDtypeStruct((1, C, 2 * C), F32),
        ),
        in_specs=[hbm] * 3,
        out_specs=(hbm, hbm, hbm),
        scratch_shapes=[
            pltpu.VMEM((4, C, PIX), BF16),
            pltpu.VMEM((4, padded, 3 * C), BF16),
            pltpu.VMEM((4, 2, 8, HALF), F32),
            pltpu.VMEM((9, C, C), F32),
            pltpu.VMEM((1, C), F32),
            pltpu.VMEM((C, 2 * C), F32),
            pltpu.SemaphoreType.DMA((28,)),
        ],
        compiler_params=pltpu.CompilerParams(vmem_limit_bytes=56 * 1024 * 1024),
    )(*chain)
    if n_dp != 2:
        grads = lax.psum(grads, "dp")
    return grads


def solution(mesh):
    in_specs = (
        P("dp", "space", None, None),
        P("dp"),
        P("dp", "space", None, None),
        P("section", None, None, None, None),
        P("section", None),
        P("section", None, None),
    )
    out_specs = (P("section", None, None, None, None), P("section", None), P("section", None, None))
    return jax.shard_map(
        per_device, mesh=mesh, in_specs=in_specs, out_specs=out_specs, check_vma=False
    )
```

```python
import functools
import math

import jax
import jax.numpy as jnp
import numpy as np
from jax import lax
from jax.experimental import pallas as pl
from jax.experimental.pallas import tpu as pltpu
from jax.sharding import PartitionSpec as P

G = 32
EPS = 1e-05
MESH = pl.DeviceIdType.MESH
F32 = jnp.float32
BF16 = jnp.bfloat16
PIX = 256
COLS = 64
C = 256
HALF = 128


def thirds(x):
    first = x.astype(BF16)
    rest = x - first.astype(F32)
    second = rest.astype(BF16)
    return first, second, (rest - second.astype(F32)).astype(BF16)


def rows_of(*rows):
    index = lax.broadcasted_iota(jnp.int32, (8, rows[0].shape[1]), 0)
    out = jnp.zeros((8, rows[0].shape[1]), F32)
    for i, row in enumerate(rows):
        out = jnp.where(index == i, row, out)
    return out


def half_at(index):
    return pl.ds(pl.multiple_of(index * HALF, HALF), HALF)


def group_means(first, second, same, scale):
    parts = [p.astype(F32) for p in thirds(first) + thirds(second)]
    sums = jnp.dot(rows_of(*parts).astype(BF16), same, preferred_element_type=F32) * scale
    return sums[0:1] + (sums[1:2] + sums[2:3]), sums[3:4] + (sums[4:5] + sums[5:6])


def spread_columns(ref, value, half):
    column = lax.broadcasted_iota(jnp.int32, (PIX, HALF), 0) & (COLS - 1)
    left = jnp.where(column == 0, 0.0, pltpu.roll(value, 1, 0))
    right = jnp.where(column == COLS - 1, 0.0, pltpu.roll(value, PIX - 1, 0))
    for kx, moved in enumerate((left, value, right)):
        ref[COLS : COLS + PIX, half_at(2 * kx + half)] = moved.astype(BF16)


def clear_border(ref):
    blank = jnp.zeros((COLS, 3 * C), BF16)
    ref[0:COLS, :] = blank
    ref[COLS + PIX : 2 * COLS + PIX, :] = blank


def convolve(ref, kernel, half):
    left = jnp.concatenate(
        [
            ref[ky * COLS : ky * COLS + PIX, half_at(2 * kx + half)]
            for ky in range(3)
            for kx in range(3)
        ],
        axis=1,
    )
    right = kernel[:, :, half_at(half), :].reshape(9 * HALF, HALF)
    return jnp.dot(left, right, preferred_element_type=F32)


def chain_body(
    n_sec, flips, steps, freqs, images, out_grad, weight, gain, emb,
    act_out, cols_out, small_out,
    act_t, g_cols, small, hbuf, skip, gskip, obuf, dbuf, act_raw, g_all, plain, across, turned, act_cols,
    normed, slope, d_act, steps_v, freqs_v, gain_v, emb_v, send, recv, local, leave,
):
    dp = lax.axis_index("dp")
    s = lax.axis_index("section")
    space = lax.axis_index("space")
    y = space // 2
    core = lax.rem(space, 2)
    last = n_sec - 1
    me = dp * 2 + y if len(flips) == 3 else y
    ahead, behind = lax.rem(s + 1, n_sec), lax.rem(s + n_sec - 1, n_sec)
    sibling = {"space": space ^ 1}

    def plane_peer(k, flip_core=0):
        return {"dp": dp ^ (k & 1), "space": space ^ (k & 2) ^ flip_core}

    others = [(k, f) for k in (0,) + flips for f in (0, 1) if k or f]
    barrier = pltpu.get_barrier_semaphore()
    partners = [plane_peer(k, f) if k & 1 else {"space": space ^ (k & 2) ^ f} for k, f in others]
    partners += [{"section": ahead}, {"section": behind}]
    for partner in partners:
        pl.semaphore_signal(barrier, inc=1, device_id=partner, device_id_type=MESH)

    loads = [
        pltpu.make_async_copy(src, dst, local.at[i])
        for i, (src, dst) in enumerate((
            (steps, steps_v),
            (freqs, freqs_v),
            (emb.at[0, :, half_at(core)], emb_v.at[0]),
            (emb.at[0, :, half_at(core + 2)], emb_v.at[1]),
            (gain.at[:, half_at(core)], gain_v),
            (weight.at[0, :, :, :, half_at(core)], plain),
            (weight.at[0, :, :, half_at(core), :], across),
        ))
    ]
    for load in loads:
        load.start()

    def remote(src, dst, number, device):
        return pltpu.make_async_remote_copy(
            src_ref=src, dst_ref=dst, send_sem=send.at[number], recv_sem=recv.at[number],
            device_id=device, device_id_type=MESH,
        )

    def row_at(index):
        return pl.ds(pl.multiple_of(index * COLS, COLS), COLS)

    g_mine = g_all.at[me, core]
    g_cols_mine = g_cols.at[me]
    act_rows = half_at(core)

    def image_row(k):
        target = space ^ k
        return remote(
            images.at[target // 2, 0, :, half_at(lax.rem(target, 2))],
            hbuf.at[row_at(space), :], k - 1, {"space": target},
        )

    def grad_row(k):
        target = space ^ k
        return remote(
            out_grad.at[target // 2, 0, :, half_at(lax.rem(target, 2))],
            g_all.at[me ^ (k >> 1), lax.rem(target, 2), row_at(space), :],
            k - 1, {"space": target},
        )

    own_image = pltpu.make_async_copy(
        images.at[y, 0, :, half_at(core)], hbuf.at[row_at(space), :], local.at[7]
    )
    own_grad = pltpu.make_async_copy(
        out_grad.at[y, 0, :, half_at(core)], g_all.at[me, core, row_at(space), :], local.at[7]
    )
    forward_hop = remote(obuf, hbuf, 3, {"section": ahead})
    forward_skip = remote(obuf, skip, 4, {"section": behind})
    backward_hop = remote(dbuf, g_mine, 5, {"section": behind})
    backward_skip = remote(dbuf, gskip, 6, {"section": ahead})
    act_sibling = remote(act_raw.at[core], act_raw.at[core], 7, sibling)
    g_sibling = remote(g_mine, g_mine, 8, sibling)
    act_copy, g_copy, act_pass, g_pass, slot = {}, {}, {}, {}, {}
    for k in flips:
        slot[k] = me ^ (((k & 1) << 1) | (k >> 1))
        mine = act_t.at[me, act_rows, :]
        theirs = act_t.at[slot[k], act_rows, :]
        act_copy[k] = remote(mine, mine, 8 + k, plane_peer(k))
        g_copy[k] = remote(g_mine, g_mine, 11 + k, plane_peer(k))
        act_pass[k] = remote(theirs, theirs, 14 + k, sibling)
        passed = g_all.at[slot[k], core]
        g_pass[k] = remote(passed, passed, 17 + k, sibling)
    small_copy = [
        remote(small.at[me, core], small.at[me, core], 21 + i, plane_peer(k, f))
        for i, (k, f) in enumerate(others)
    ]

    for load in loads[:5]:
        load.wait()
    angles = steps_v[y].astype(F32) * freqs_v[...]
    cosines, sines = jnp.cos(angles), jnp.sin(angles)
    features = jnp.concatenate([cosines, sines], axis=1)
    features = rows_of(*[p.astype(F32) for p in thirds(features)]).astype(BF16)
    scales1, shifts = (
        part[0:1] + (part[1:2] + part[2:3])
        for part in (
            jnp.dot(features, emb_v[i], preferred_element_type=F32) for i in range(2)
        )
    )
    scales1 = 1.0 + scales1
    gains = gain_v[...]
    factor = gains * scales1

    clear_border(act_cols)
    for i in range(4):
        clear_border(g_cols.at[i])
    same = (
        lax.broadcasted_iota(jnp.int32, (HALF, HALF), 0) // (C // G)
        == lax.broadcasted_iota(jnp.int32, (HALF, HALF), 1) // (C // G)
    ).astype(F32).astype(BF16)
    cells = PIX * (C // G)

    pl.semaphore_wait(barrier, len(partners))

    @pl.when(s == 0)
    def _():
        for k in (1, 2, 3):
            image_row(k).start()
        own_image.start()

    @pl.when(s == last)
    def _():
        for k in (1, 2, 3):
            grad_row(k).start()
        own_grad.start()

    for load in loads[5:]:
        load.wait()

    def turn_weights():
        for ky in range(3):
            for kx in range(3):
                turned[ky, kx] = across[2 - ky, 2 - kx].T

    def back_convolve():
        g_sibling.start()
        spread_columns(g_cols_mine, g_mine[...].astype(F32), core)
        total = convolve(g_cols_mine, turned, core)
        g_sibling.wait_recv()
        spread_columns(g_cols_mine, g_all[me, 1 - core].astype(F32), 1 - core)
        d_act[...] = total + convolve(g_cols_mine, turned, 1 - core)

    @pl.when(s == 0)
    def _():
        own_image.wait()
        for k in (1, 2, 3):
            image_row(k).wait_recv()

    @pl.when(s == last)
    def _():
        turn_weights()
        own_grad.wait()
        for k in (1, 2, 3):
            grad_row(k).wait_recv()
        back_convolve()

    @pl.when(s > 0)
    def _():
        forward_hop.wait_recv()

    @pl.when(s == last)
    def _():
        forward_skip.wait_recv()
        hbuf[...] = (hbuf[...].astype(F32) + skip[...].astype(F32)).astype(BF16)

    tensor = hbuf[...].astype(F32)
    first = jnp.sum(tensor, axis=0, keepdims=True)
    square = jnp.sum(tensor * tensor, axis=0, keepdims=True)
    average, mean_square = group_means(first, square, same, 1.0 / cells)
    inverse = lax.rsqrt(mean_square - average * average + EPS)
    normal = (tensor - average) * inverse
    normed[...] = normal
    pre = normal * factor + shifts
    sigmoid = jax.nn.sigmoid(pre)
    act = pre * sigmoid
    act_raw[core] = act.astype(BF16)
    act_sibling.start()

    @pl.when(s < last)
    def _():
        spread_columns(act_cols, act, core)
        out = hbuf[...].astype(F32) + convolve(act_cols, plain, core)
        act_sibling.wait_recv()
        spread_columns(act_cols, act_raw[1 - core].astype(F32), 1 - core)
        obuf[...] = (out + convolve(act_cols, plain, 1 - core)).astype(BF16)
        forward_hop.start()

    @pl.when(s == 0)
    def _():
        forward_skip.start()

    slope[...] = sigmoid * (1.0 + pre * (1.0 - sigmoid))

    def share_act():
        act_t[me, act_rows, :] = act_raw[core].T
        for k in flips:
            act_copy[k].start()
        act_t[me, half_at(1 - core), :] = act_raw[1 - core].T

    @pl.when(s < last)
    def _():
        share_act()
        turn_weights()
        backward_hop.wait_recv()

    @pl.when(s == 0)
    def _():
        backward_skip.wait_recv()
        g_all[me, core] = (g_mine[...].astype(F32) + gskip[...].astype(F32)).astype(BF16)

    def share_grad():
        for k in reversed(flips):
            g_copy[k].start()

    @pl.when(s == 0)
    def _():
        share_grad()

    @pl.when(s < last)
    def _():
        back_convolve()

    d_pre = d_act[...] * slope[...]
    normal = normed[...]
    sum_pre = jnp.sum(d_pre, axis=0, keepdims=True)
    sum_normal = jnp.sum(d_pre * normal, axis=0, keepdims=True)

    @pl.when(s > 0)
    def _():
        mean_d, mean_dn = group_means(sum_pre * factor, sum_normal * factor, same, 1.0 / cells)
        d_tensor = inverse * (d_pre * factor - mean_d - normal * mean_dn)
        dbuf[...] = (g_mine[...].astype(F32) + d_tensor).astype(BF16)
        backward_hop.start()
        share_grad()

    @pl.when(s == last)
    def _():
        backward_skip.start()
        act_sibling.wait_recv()
        share_act()

    small[me, core] = rows_of(sum_normal * gains, sum_pre, sum_normal * scales1, cosines, sines)
    for copy in small_copy:
        copy.start()

    def image_out(slot_no, number):
        return [
            pltpu.make_async_copy(act_t.at[slot_no], act_out.at[slot_no], leave.at[number]),
            pltpu.make_async_copy(g_cols.at[slot_no], cols_out.at[slot_no], leave.at[4 + number]),
        ]

    leaving = image_out(me, 0)
    for copy in leaving:
        copy.start()

    for k in flips:
        act_copy[k].wait_recv()
        act_pass[k].start()
    for k in flips:
        g_copy[k].wait_recv()
        g_pass[k].start()
        spread_columns(g_cols.at[slot[k]], g_all[slot[k], core].astype(F32), core)
    for k in flips:
        act_pass[k].wait_recv()
        g_pass[k].wait_recv()
        spread_columns(g_cols.at[slot[k]], g_all[slot[k], 1 - core].astype(F32), 1 - core)
        for copy in image_out(slot[k], k):
            copy.start()
            leaving.append(copy)
    for copy in small_copy:
        copy.wait_recv()
    leaving.append(pltpu.make_async_copy(small, small_out, leave.at[8]))
    leaving[-1].start()

    @pl.when(s == 0)
    def _():
        for k in (1, 2, 3):
            image_row(k).wait_send()
        forward_skip.wait_send()

    @pl.when(s == last)
    def _():
        for k in (1, 2, 3):
            grad_row(k).wait_send()
        backward_skip.wait_send()

    @pl.when(s < last)
    def _():
        forward_hop.wait_send()

    @pl.when(s > 0)
    def _():
        backward_hop.wait_send()

    act_sibling.wait_send()
    g_sibling.wait_send()
    for k in flips:
        for copy in (act_copy[k], g_copy[k], act_pass[k], g_pass[k]):
            copy.wait_send()
    for copy in small_copy:
        copy.wait_send()
    for copy in leaving:
        copy.wait()


def grad_body(
    slots, act_in, cols_in, small_in, conv_out, gain_out, emb_out,
    act_t, g_cols, small, taps, gain_v, emb_v, sems,
):
    loads = [pltpu.make_async_copy(small_in, small, sems.at[11])]
    for i in range(slots):
        loads.append(pltpu.make_async_copy(act_in.at[i], act_t.at[i], sems.at[12 + i]))
        loads.append(pltpu.make_async_copy(cols_in.at[i], g_cols.at[i], sems.at[16 + i]))
    for load in loads:
        load.start()
    loads[0].wait()
    packed = [jnp.concatenate([small[i, 0], small[i, 1]], axis=1) for i in range(slots)]
    gain_total = packed[0][2:3]
    for block in packed[1:]:
        gain_total = gain_total + block[2:3]
    gain_v[...] = gain_total
    features = rows_of(
        *[jnp.concatenate([small[i, 0, 3:4], small[i, 0, 4:5]], axis=1) for i in range(slots)]
    )
    d_rows = rows_of(*[jnp.concatenate([block[0:1], block[1:2]], axis=1) for block in packed])
    emb_v[...] = jnp.dot(
        features.T, d_rows, precision=lax.Precision.HIGHEST, preferred_element_type=F32
    )
    copies = [
        pltpu.make_async_copy(gain_v, gain_out, sems.at[9]),
        pltpu.make_async_copy(emb_v, emb_out.at[0], sems.at[10]),
    ]
    for copy in copies:
        copy.start()
    for load in loads[1:]:
        load.wait()
    left = jnp.concatenate([act_t[i] for i in range(slots)], axis=1)
    for ky in range(3):
        for kx in range(3):
            rows, lanes = slice(ky * COLS, ky * COLS + PIX), slice(kx * C, (kx + 1) * C)
            right = jnp.concatenate([g_cols[i, rows, lanes] for i in range(slots)], axis=0)
            total = jnp.dot(left, right, preferred_element_type=F32)
            tap = ky * 3 + kx
            taps[tap] = total
            copy = pltpu.make_async_copy(taps.at[tap], conv_out.at[0, 2 - ky, 2 - kx], sems.at[tap])
            copy.start()
            copies.append(copy)
    for copy in copies:
        copy.wait()


def per_device(images, steps, out_grad, conv_weight, gn_gain, emb_weight):
    n_dp = lax.axis_size("dp")
    n_sec = lax.axis_size("section")
    flips = (1, 2, 3) if n_dp == 2 else (2,)
    half = C // 2
    freqs = np.exp(-math.log(10000.0) * np.arange(half, dtype=np.float32) / half)
    hbm = pl.BlockSpec(memory_space=pltpu.HBM)
    padded = PIX + 2 * COLS
    chain = pl.pallas_call(
        functools.partial(chain_body, n_sec, flips),
        out_shape=(
            jax.ShapeDtypeStruct((4, C, PIX), BF16),
            jax.ShapeDtypeStruct((4, padded, 3 * C), BF16),
            jax.ShapeDtypeStruct((4, 2, 8, HALF), F32),
        ),
        in_specs=[hbm] * 7,
        out_specs=(hbm, hbm, hbm),
        scratch_shapes=[
            pltpu.VMEM((4, C, PIX), BF16),
            pltpu.VMEM((4, padded, 3 * C), BF16),
            pltpu.VMEM((4, 2, 8, HALF), F32),
            pltpu.VMEM((PIX, HALF), BF16),
            pltpu.VMEM((PIX, HALF), BF16),
            pltpu.VMEM((PIX, HALF), BF16),
            pltpu.VMEM((PIX, HALF), BF16),
            pltpu.VMEM((PIX, HALF), BF16),
            pltpu.VMEM((2, PIX, HALF), BF16),
            pltpu.VMEM((4, 2, PIX, HALF), BF16),
            pltpu.VMEM((3, 3, C, HALF), BF16),
            pltpu.VMEM((3, 3, HALF, C), BF16),
            pltpu.VMEM((3, 3, C, HALF), BF16),
            pltpu.VMEM((padded, 3 * C), BF16),
            pltpu.VMEM((PIX, HALF), F32),
            pltpu.VMEM((PIX, HALF), F32),
            pltpu.VMEM((PIX, HALF), F32),
            pltpu.SMEM((2,), jnp.int32),
            pltpu.VMEM((1, HALF), F32),
            pltpu.VMEM((1, HALF), F32),
            pltpu.VMEM((2, C, HALF), BF16),
            pltpu.SemaphoreType.DMA((28,)),
            pltpu.SemaphoreType.DMA((28,)),
            pltpu.SemaphoreType.DMA((8,)),
            pltpu.SemaphoreType.DMA((9,)),
        ],
        compiler_params=pltpu.CompilerParams(
            collective_id=0, has_side_effects=True, vmem_limit_bytes=56 * 1024 * 1024
        ),
    )(
        steps, jnp.asarray(freqs, F32)[None, :], images, out_grad, conv_weight, gn_gain, emb_weight
    )
    grads = pl.pallas_call(
        functools.partial(grad_body, 4 if n_dp == 2 else 2),
        out_shape=(
            jax.ShapeDtypeStruct((1, 3, 3, C, C), F32),
            jax.ShapeDtypeStruct((1, C), F32),
            jax.ShapeDtypeStruct((1, C, 2 * C), F32),
        ),
        in_specs=[hbm] * 3,
        out_specs=(hbm, hbm, hbm),
        scratch_shapes=[
            pltpu.VMEM((4, C, PIX), BF16),
            pltpu.VMEM((4, padded, 3 * C), BF16),
            pltpu.VMEM((4, 2, 8, HALF), F32),
            pltpu.VMEM((9, C, C), F32),
            pltpu.VMEM((1, C), F32),
            pltpu.VMEM((C, 2 * C), F32),
            pltpu.SemaphoreType.DMA((20,)),
        ],
        compiler_params=pltpu.CompilerParams(vmem_limit_bytes=56 * 1024 * 1024),
    )(*chain)
    if n_dp != 2:
        grads = lax.psum(grads, "dp")
    return grads


def solution(mesh):
    in_specs = (
        P("dp", "space", None, None),
        P("dp"),
        P("dp", "space", None, None),
        P("section", None, None, None, None),
        P("section", None),
        P("section", None, None),
    )
    out_specs = (P("section", None, None, None, None), P("section", None), P("section", None, None))
    return jax.shard_map(
        per_device, mesh=mesh, in_specs=in_specs, out_specs=out_specs, check_vma=False
    )
```

```python
import functools
import math

import jax
import jax.numpy as jnp
import numpy as np
from jax import lax
from jax.experimental import pallas as pl
from jax.experimental.pallas import tpu as pltpu
from jax.sharding import PartitionSpec as P

G = 32
EPS = 1e-05
MESH = pl.DeviceIdType.MESH
F32 = jnp.float32
BF16 = jnp.bfloat16
PIX = 256
COLS = 64
C = 256
HALF = 128


def thirds(x):
    first = x.astype(BF16)
    rest = x - first.astype(F32)
    second = rest.astype(BF16)
    return first, second, (rest - second.astype(F32)).astype(BF16)


def rows_of(*rows):
    index = lax.broadcasted_iota(jnp.int32, (8, rows[0].shape[1]), 0)
    out = jnp.zeros((8, rows[0].shape[1]), F32)
    for i, row in enumerate(rows):
        out = jnp.where(index == i, row, out)
    return out


def half_at(index):
    return pl.ds(pl.multiple_of(index * HALF, HALF), HALF)


def group_means(first, second, same, scale):
    parts = [p.astype(F32) for p in thirds(first) + thirds(second)]
    sums = jnp.dot(rows_of(*parts).astype(BF16), same, preferred_element_type=F32) * scale
    return sums[0:1] + (sums[1:2] + sums[2:3]), sums[3:4] + (sums[4:5] + sums[5:6])


def spread_columns(ref, value, half):
    column = lax.broadcasted_iota(jnp.int32, (PIX, HALF), 0) & (COLS - 1)
    left = jnp.where(column == 0, 0.0, pltpu.roll(value, 1, 0))
    right = jnp.where(column == COLS - 1, 0.0, pltpu.roll(value, PIX - 1, 0))
    for kx, moved in enumerate((left, value, right)):
        ref[COLS : COLS + PIX, half_at(2 * kx + half)] = moved.astype(BF16)


def clear_border(ref):
    blank = jnp.zeros((COLS, 3 * C), BF16)
    ref[0:COLS, :] = blank
    ref[COLS + PIX : 2 * COLS + PIX, :] = blank


def convolve(ref, kernel, half):
    left = jnp.concatenate(
        [
            ref[ky * COLS : ky * COLS + PIX, half_at(2 * kx + half)]
            for ky in range(3)
            for kx in range(3)
        ],
        axis=1,
    )
    right = kernel[:, :, half_at(half), :].reshape(9 * HALF, HALF)
    return jnp.dot(left, right, preferred_element_type=F32)


def chain_body(
    n_sec, flips, steps, freqs, images, out_grad, weight, gain, emb,
    act_out, cols_out, small_out,
    act_t, g_cols, small, hbuf, skip, gskip, obuf, dbuf, act_raw, g_all, plain, across, turned, act_cols,
    normed, slope, d_act, steps_v, freqs_v, gain_v, emb_v, send, recv, local, leave,
):
    dp = lax.axis_index("dp")
    s = lax.axis_index("section")
    space = lax.axis_index("space")
    y = space // 2
    core = lax.rem(space, 2)
    last = n_sec - 1
    me = dp * 2 + y if len(flips) == 3 else y
    ahead, behind = lax.rem(s + 1, n_sec), lax.rem(s + n_sec - 1, n_sec)
    sibling = {"space": space ^ 1}

    def plane_peer(k, flip_core=0):
        return {"dp": dp ^ (k & 1), "space": space ^ (k & 2) ^ flip_core}

    others = [(k, f) for k in (0,) + flips for f in (0, 1) if k or f]
    barrier = pltpu.get_barrier_semaphore()
    partners = [plane_peer(k, f) if k & 1 else {"space": space ^ (k & 2) ^ f} for k, f in others]
    partners += [{"section": ahead}, {"section": behind}]
    for partner in partners:
        pl.semaphore_signal(barrier, inc=1, device_id=partner, device_id_type=MESH)

    loads = [
        pltpu.make_async_copy(src, dst, local.at[i])
        for i, (src, dst) in enumerate((
            (steps, steps_v),
            (freqs, freqs_v),
            (emb.at[0, :, half_at(core)], emb_v.at[0]),
            (emb.at[0, :, half_at(core + 2)], emb_v.at[1]),
            (gain.at[:, half_at(core)], gain_v),
            (weight.at[0, :, :, :, half_at(core)], plain),
            (weight.at[0, :, :, half_at(core), :], across),
        ))
    ]
    for load in loads:
        load.start()

    def remote(src, dst, number, device):
        return pltpu.make_async_remote_copy(
            src_ref=src, dst_ref=dst, send_sem=send.at[number], recv_sem=recv.at[number],
            device_id=device, device_id_type=MESH,
        )

    def row_at(index):
        return pl.ds(pl.multiple_of(index * COLS, COLS), COLS)

    g_mine = g_all.at[me, core]
    g_cols_mine = g_cols.at[me]
    act_rows = half_at(core)

    def image_row(k):
        target = space ^ k
        return remote(
            images.at[target // 2, 0, :, half_at(lax.rem(target, 2))],
            hbuf.at[row_at(space), :], k - 1, {"space": target},
        )

    def grad_row(k):
        target = space ^ k
        return remote(
            out_grad.at[target // 2, 0, :, half_at(lax.rem(target, 2))],
            g_all.at[me ^ (k >> 1), lax.rem(target, 2), row_at(space), :],
            k - 1, {"space": target},
        )

    own_image = pltpu.make_async_copy(
        images.at[y, 0, :, half_at(core)], hbuf.at[row_at(space), :], local.at[7]
    )
    own_grad = pltpu.make_async_copy(
        out_grad.at[y, 0, :, half_at(core)], g_all.at[me, core, row_at(space), :], local.at[7]
    )
    forward_hop = remote(obuf, hbuf, 3, {"section": ahead})
    forward_skip = remote(obuf, skip, 4, {"section": behind})
    backward_hop = remote(dbuf, g_mine, 5, {"section": behind})
    backward_skip = remote(dbuf, gskip, 6, {"section": ahead})
    act_sibling = remote(act_raw.at[core], act_raw.at[core], 7, sibling)
    g_sibling = remote(g_mine, g_mine, 8, sibling)
    act_copy, g_copy, act_pass, g_pass, slot = {}, {}, {}, {}, {}
    for k in flips:
        slot[k] = me ^ (((k & 1) << 1) | (k >> 1))
        mine = act_t.at[me, act_rows, :]
        theirs = act_t.at[slot[k], act_rows, :]
        act_copy[k] = remote(mine, mine, 8 + k, plane_peer(k))
        g_copy[k] = remote(g_mine, g_mine, 11 + k, plane_peer(k))
        act_pass[k] = remote(theirs, theirs, 14 + k, sibling)
        passed = g_all.at[slot[k], core]
        g_pass[k] = remote(passed, passed, 17 + k, sibling)
    small_copy = [
        remote(small.at[me, core], small.at[me, core], 21 + i, plane_peer(k, f))
        for i, (k, f) in enumerate(others)
    ]

    for load in loads[:5]:
        load.wait()
    angles = steps_v[y].astype(F32) * freqs_v[...]
    cosines, sines = jnp.cos(angles), jnp.sin(angles)
    features = jnp.concatenate([cosines, sines], axis=1)
    features = rows_of(*[p.astype(F32) for p in thirds(features)]).astype(BF16)
    scales1, shifts = (
        part[0:1] + (part[1:2] + part[2:3])
        for part in (
            jnp.dot(features, emb_v[i], preferred_element_type=F32) for i in range(2)
        )
    )
    scales1 = 1.0 + scales1
    gains = gain_v[...]
    factor = gains * scales1

    clear_border(act_cols)
    for i in range(4):
        clear_border(g_cols.at[i])
    same = (
        lax.broadcasted_iota(jnp.int32, (HALF, HALF), 0) // (C // G)
        == lax.broadcasted_iota(jnp.int32, (HALF, HALF), 1) // (C // G)
    ).astype(F32).astype(BF16)
    cells = PIX * (C // G)

    pl.semaphore_wait(barrier, len(partners))

    @pl.when(s == 0)
    def _():
        for k in (1, 2, 3):
            image_row(k).start()
        own_image.start()

    @pl.when(s == last)
    def _():
        for k in (1, 2, 3):
            grad_row(k).start()
        own_grad.start()

    for load in loads[5:]:
        load.wait()

    def turn_weights():
        for ky in range(3):
            for kx in range(3):
                turned[ky, kx] = across[2 - ky, 2 - kx].T

    def back_convolve():
        g_sibling.start()
        spread_columns(g_cols_mine, g_mine[...].astype(F32), core)
        total = convolve(g_cols_mine, turned, core)
        g_sibling.wait_recv()
        spread_columns(g_cols_mine, g_all[me, 1 - core].astype(F32), 1 - core)
        d_act[...] = total + convolve(g_cols_mine, turned, 1 - core)

    @pl.when(s == 0)
    def _():
        own_image.wait()
        for k in (1, 2, 3):
            image_row(k).wait_recv()

    @pl.when(s == last)
    def _():
        turn_weights()
        own_grad.wait()
        for k in (1, 2, 3):
            grad_row(k).wait_recv()
        back_convolve()

    @pl.when(s > 0)
    def _():
        forward_hop.wait_recv()

    @pl.when(s == last)
    def _():
        forward_skip.wait_recv()
        hbuf[...] = (hbuf[...].astype(F32) + skip[...].astype(F32)).astype(BF16)

    tensor = hbuf[...].astype(F32)
    first = jnp.sum(tensor, axis=0, keepdims=True)
    square = jnp.sum(tensor * tensor, axis=0, keepdims=True)
    average, mean_square = group_means(first, square, same, 1.0 / cells)
    inverse = lax.rsqrt(mean_square - average * average + EPS)
    normal = (tensor - average) * inverse
    normed[...] = normal
    pre = normal * factor + shifts
    sigmoid = jax.nn.sigmoid(pre)
    act = pre * sigmoid
    act_raw[core] = act.astype(BF16)
    act_sibling.start()

    @pl.when(s < last)
    def _():
        spread_columns(act_cols, act, core)
        out = hbuf[...].astype(F32) + convolve(act_cols, plain, core)
        act_sibling.wait_recv()
        spread_columns(act_cols, act_raw[1 - core].astype(F32), 1 - core)
        obuf[...] = (out + convolve(act_cols, plain, 1 - core)).astype(BF16)
        forward_hop.start()

    slope[...] = sigmoid * (1.0 + pre * (1.0 - sigmoid))

    def share_act():
        act_t[me, act_rows, :] = act_raw[core].T
        for k in flips:
            act_copy[k].start()
        act_t[me, half_at(1 - core), :] = act_raw[1 - core].T

    @pl.when(s < last)
    def _():
        share_act()
        turn_weights()
        forward_hop.wait_send()

    @pl.when(s == 0)
    def _():
        forward_skip.start()

    @pl.when(s < last)
    def _():
        backward_hop.wait_recv()

    @pl.when(s == 0)
    def _():
        backward_skip.wait_recv()
        g_all[me, core] = (g_mine[...].astype(F32) + gskip[...].astype(F32)).astype(BF16)

    def share_grad():
        for k in reversed(flips):
            g_copy[k].start()

    @pl.when(s == 0)
    def _():
        share_grad()

    @pl.when(s < last)
    def _():
        back_convolve()

    d_pre = d_act[...] * slope[...]
    normal = normed[...]
    sum_pre = jnp.sum(d_pre, axis=0, keepdims=True)
    sum_normal = jnp.sum(d_pre * normal, axis=0, keepdims=True)

    @pl.when(s > 0)
    def _():
        mean_d, mean_dn = group_means(sum_pre * factor, sum_normal * factor, same, 1.0 / cells)
        d_tensor = inverse * (d_pre * factor - mean_d - normal * mean_dn)
        dbuf[...] = (g_mine[...].astype(F32) + d_tensor).astype(BF16)
        backward_hop.start()
        share_grad()

    @pl.when(s == last)
    def _():
        act_sibling.wait_recv()
        share_act()
        backward_hop.wait_send()
        backward_skip.start()

    small[me, core] = rows_of(sum_normal * gains, sum_pre, sum_normal * scales1, cosines, sines)
    for copy in small_copy:
        copy.start()

    def image_out(slot_no, number):
        return [
            pltpu.make_async_copy(act_t.at[slot_no], act_out.at[slot_no], leave.at[number]),
            pltpu.make_async_copy(g_cols.at[slot_no], cols_out.at[slot_no], leave.at[4 + number]),
        ]

    leaving = image_out(me, 0)
    for copy in leaving:
        copy.start()

    for k in flips:
        act_copy[k].wait_recv()
        act_pass[k].start()
    for k in flips:
        g_copy[k].wait_recv()
        g_pass[k].start()
        spread_columns(g_cols.at[slot[k]], g_all[slot[k], core].astype(F32), core)
    for k in flips:
        act_pass[k].wait_recv()
        g_pass[k].wait_recv()
        spread_columns(g_cols.at[slot[k]], g_all[slot[k], 1 - core].astype(F32), 1 - core)
        for copy in image_out(slot[k], k):
            copy.start()
            leaving.append(copy)
    for copy in small_copy:
        copy.wait_recv()
    leaving.append(pltpu.make_async_copy(small, small_out, leave.at[8]))
    leaving[-1].start()

    @pl.when(s == 0)
    def _():
        for k in (1, 2, 3):
            image_row(k).wait_send()
        forward_skip.wait_send()

    @pl.when(s == last)
    def _():
        for k in (1, 2, 3):
            grad_row(k).wait_send()
        backward_skip.wait_send()

    @pl.when((s > 0) & (s < last))
    def _():
        backward_hop.wait_send()

    act_sibling.wait_send()
    g_sibling.wait_send()
    for k in flips:
        for copy in (act_copy[k], g_copy[k], act_pass[k], g_pass[k]):
            copy.wait_send()
    for copy in small_copy:
        copy.wait_send()
    for copy in leaving:
        copy.wait()


def grad_body(
    slots, act_in, cols_in, small_in, conv_out, gain_out, emb_out,
    act_t, g_cols, small, taps, gain_v, emb_v, sems,
):
    loads = [pltpu.make_async_copy(small_in, small, sems.at[11])]
    for i in range(slots):
        loads.append(pltpu.make_async_copy(act_in.at[i], act_t.at[i], sems.at[12 + i]))
        loads.append(pltpu.make_async_copy(cols_in.at[i], g_cols.at[i], sems.at[16 + i]))
    for load in loads:
        load.start()
    loads[0].wait()
    packed = [jnp.concatenate([small[i, 0], small[i, 1]], axis=1) for i in range(slots)]
    gain_total = packed[0][2:3]
    for block in packed[1:]:
        gain_total = gain_total + block[2:3]
    gain_v[...] = gain_total
    features = rows_of(
        *[jnp.concatenate([small[i, 0, 3:4], small[i, 0, 4:5]], axis=1) for i in range(slots)]
    )
    d_rows = rows_of(*[jnp.concatenate([block[0:1], block[1:2]], axis=1) for block in packed])
    emb_v[...] = jnp.dot(
        features.T, d_rows, precision=lax.Precision.HIGHEST, preferred_element_type=F32
    )
    copies = [
        pltpu.make_async_copy(gain_v, gain_out, sems.at[9]),
        pltpu.make_async_copy(emb_v, emb_out.at[0], sems.at[10]),
    ]
    for copy in copies:
        copy.start()
    for load in loads[1:]:
        load.wait()
    left = jnp.concatenate([act_t[i] for i in range(slots)], axis=1)
    for ky in range(3):
        for kx in range(3):
            rows, lanes = slice(ky * COLS, ky * COLS + PIX), slice(kx * C, (kx + 1) * C)
            right = jnp.concatenate([g_cols[i, rows, lanes] for i in range(slots)], axis=0)
            total = jnp.dot(left, right, preferred_element_type=F32)
            tap = ky * 3 + kx
            taps[tap] = total
            copy = pltpu.make_async_copy(taps.at[tap], conv_out.at[0, 2 - ky, 2 - kx], sems.at[tap])
            copy.start()
            copies.append(copy)
    for copy in copies:
        copy.wait()


def per_device(images, steps, out_grad, conv_weight, gn_gain, emb_weight):
    n_dp = lax.axis_size("dp")
    n_sec = lax.axis_size("section")
    flips = (1, 2, 3) if n_dp == 2 else (2,)
    half = C // 2
    freqs = np.exp(-math.log(10000.0) * np.arange(half, dtype=np.float32) / half)
    hbm = pl.BlockSpec(memory_space=pltpu.HBM)
    padded = PIX + 2 * COLS
    chain = pl.pallas_call(
        functools.partial(chain_body, n_sec, flips),
        out_shape=(
            jax.ShapeDtypeStruct((4, C, PIX), BF16),
            jax.ShapeDtypeStruct((4, padded, 3 * C), BF16),
            jax.ShapeDtypeStruct((4, 2, 8, HALF), F32),
        ),
        in_specs=[hbm] * 7,
        out_specs=(hbm, hbm, hbm),
        scratch_shapes=[
            pltpu.VMEM((4, C, PIX), BF16),
            pltpu.VMEM((4, padded, 3 * C), BF16),
            pltpu.VMEM((4, 2, 8, HALF), F32),
            pltpu.VMEM((PIX, HALF), BF16),
            pltpu.VMEM((PIX, HALF), BF16),
            pltpu.VMEM((PIX, HALF), BF16),
            pltpu.VMEM((PIX, HALF), BF16),
            pltpu.VMEM((PIX, HALF), BF16),
            pltpu.VMEM((2, PIX, HALF), BF16),
            pltpu.VMEM((4, 2, PIX, HALF), BF16),
            pltpu.VMEM((3, 3, C, HALF), BF16),
            pltpu.VMEM((3, 3, HALF, C), BF16),
            pltpu.VMEM((3, 3, C, HALF), BF16),
            pltpu.VMEM((padded, 3 * C), BF16),
            pltpu.VMEM((PIX, HALF), F32),
            pltpu.VMEM((PIX, HALF), F32),
            pltpu.VMEM((PIX, HALF), F32),
            pltpu.SMEM((2,), jnp.int32),
            pltpu.VMEM((1, HALF), F32),
            pltpu.VMEM((1, HALF), F32),
            pltpu.VMEM((2, C, HALF), BF16),
            pltpu.SemaphoreType.DMA((28,)),
            pltpu.SemaphoreType.DMA((28,)),
            pltpu.SemaphoreType.DMA((8,)),
            pltpu.SemaphoreType.DMA((9,)),
        ],
        compiler_params=pltpu.CompilerParams(
            collective_id=0, has_side_effects=True, vmem_limit_bytes=56 * 1024 * 1024
        ),
    )(
        steps, jnp.asarray(freqs, F32)[None, :], images, out_grad, conv_weight, gn_gain, emb_weight
    )
    grads = pl.pallas_call(
        functools.partial(grad_body, 4 if n_dp == 2 else 2),
        out_shape=(
            jax.ShapeDtypeStruct((1, 3, 3, C, C), F32),
            jax.ShapeDtypeStruct((1, C), F32),
            jax.ShapeDtypeStruct((1, C, 2 * C), F32),
        ),
        in_specs=[hbm] * 3,
        out_specs=(hbm, hbm, hbm),
        scratch_shapes=[
            pltpu.VMEM((4, C, PIX), BF16),
            pltpu.VMEM((4, padded, 3 * C), BF16),
            pltpu.VMEM((4, 2, 8, HALF), F32),
            pltpu.VMEM((9, C, C), F32),
            pltpu.VMEM((1, C), F32),
            pltpu.VMEM((C, 2 * C), F32),
            pltpu.SemaphoreType.DMA((20,)),
        ],
        compiler_params=pltpu.CompilerParams(vmem_limit_bytes=56 * 1024 * 1024),
    )(*chain)
    if n_dp != 2:
        grads = lax.psum(grads, "dp")
    return grads


def solution(mesh):
    in_specs = (
        P("dp", "space", None, None),
        P("dp"),
        P("dp", "space", None, None),
        P("section", None, None, None, None),
        P("section", None),
        P("section", None, None),
    )
    out_specs = (P("section", None, None, None, None), P("section", None), P("section", None, None))
    return jax.shard_map(
        per_device, mesh=mesh, in_specs=in_specs, out_specs=out_specs, check_vma=False
    )
```

```python
import functools
import math

import jax
import jax.numpy as jnp
import numpy as np
from jax import lax
from jax.experimental import pallas as pl
from jax.experimental.pallas import tpu as pltpu
from jax.sharding import PartitionSpec as P

G = 32
EPS = 1e-05
MESH = pl.DeviceIdType.MESH
F32 = jnp.float32
BF16 = jnp.bfloat16
PIX = 256
COLS = 64
C = 256


def thirds(x):
    first = x.astype(BF16)
    rest = x - first.astype(F32)
    second = rest.astype(BF16)
    return first, second, (rest - second.astype(F32)).astype(BF16)


def rows_of(*rows):
    index = lax.broadcasted_iota(jnp.int32, (8, rows[0].shape[1]), 0)
    out = jnp.zeros((8, rows[0].shape[1]), F32)
    for i, row in enumerate(rows):
        out = jnp.where(index == i, row, out)
    return out


def group_means(first, second, same, scale):
    parts = [p.astype(F32) for p in thirds(first) + thirds(second)]
    sums = jnp.dot(rows_of(*parts).astype(BF16), same, preferred_element_type=F32) * scale
    return sums[0:1] + (sums[1:2] + sums[2:3]), sums[3:4] + (sums[4:5] + sums[5:6])


def spread_columns(ref, value):
    column = lax.broadcasted_iota(jnp.int32, (PIX, C), 0) & (COLS - 1)
    left = jnp.where(column == 0, 0.0, pltpu.roll(value, 1, 0))
    right = jnp.where(column == COLS - 1, 0.0, pltpu.roll(value, PIX - 1, 0))
    ref[COLS : COLS + PIX, 0:C] = left.astype(BF16)
    ref[COLS : COLS + PIX, C : 2 * C] = value.astype(BF16)
    ref[COLS : COLS + PIX, 2 * C : 3 * C] = right.astype(BF16)


def clear_border(ref):
    blank = jnp.zeros((COLS, 3 * C), BF16)
    ref[0:COLS, :] = blank
    ref[COLS + PIX : 2 * COLS + PIX, :] = blank


def convolve(ref, kernel):
    left = jnp.concatenate([ref[ky * COLS : ky * COLS + PIX, :] for ky in range(3)], axis=1)
    return jnp.dot(left, kernel.reshape(9 * C, C), preferred_element_type=F32)


def chain_body(
    n_sec, flips, steps, freqs, images, out_grad, weight, gain, emb,
    act_out, cols_out, small_out,
    act_t, g_cols, small, hbuf, skip, gskip, obuf, dbuf, g_all, plain, turned, act_cols,
    normed, slope, d_act, steps_v, freqs_v, gain_v, emb_v, send, recv, local, leave,
):
    dp = lax.axis_index("dp")
    s = lax.axis_index("section")
    space = lax.axis_index("space")
    y = space // 2
    last = n_sec - 1
    me = dp * 2 + y if len(flips) == 3 else y
    ahead, behind = lax.rem(s + 1, n_sec), lax.rem(s + n_sec - 1, n_sec)

    def space_peer(k):
        return {"space": space ^ k}

    def plane_peer(k):
        if k == 2:
            return {"space": space ^ 2}
        return {"dp": dp ^ 1, "space": space ^ (k & 2)}

    barrier = pltpu.get_barrier_semaphore()
    partners = [space_peer(k) for k in (1, 2, 3)]
    partners += [plane_peer(k) for k in flips if k != 2]
    partners += [{"section": ahead}, {"section": behind}]
    for partner in partners:
        pl.semaphore_signal(barrier, inc=1, device_id=partner, device_id_type=MESH)

    loads = [
        pltpu.make_async_copy(src, dst, local.at[i])
        for i, (src, dst) in enumerate((
            (steps, steps_v), (freqs, freqs_v), (emb.at[0], emb_v), (gain, gain_v),
            (weight.at[0], plain),
        ))
    ]
    for load in loads:
        load.start()

    def remote(src, dst, number, device):
        return pltpu.make_async_remote_copy(
            src_ref=src, dst_ref=dst, send_sem=send.at[number], recv_sem=recv.at[number],
            device_id=device, device_id_type=MESH,
        )

    def row_at(index):
        return pl.ds(pl.multiple_of(index * COLS, COLS), COLS)

    g_mine = g_all.at[me]
    g_cols_mine = g_cols.at[me]

    def image_row(k):
        return remote(
            images.at[(space ^ k) // 2, 0], hbuf.at[row_at(space), :], k - 1, space_peer(k)
        )

    def grad_row(k):
        return remote(
            out_grad.at[(space ^ k) // 2, 0], g_all.at[me ^ (k >> 1), row_at(space), :],
            k - 1, space_peer(k),
        )

    own_image = pltpu.make_async_copy(images.at[y, 0], hbuf.at[row_at(space), :], local.at[5])
    own_grad = pltpu.make_async_copy(
        out_grad.at[y, 0], g_all.at[me, row_at(space), :], local.at[5]
    )
    forward_hop = remote(obuf, hbuf, 3, {"section": ahead})
    forward_skip = remote(obuf, skip, 4, {"section": behind})
    backward_hop = remote(dbuf, g_mine, 5, {"section": behind})
    backward_skip = remote(dbuf, gskip, 6, {"section": ahead})
    act_copy = {k: remote(act_t.at[me], act_t.at[me], 6 + k, plane_peer(k)) for k in flips}
    g_copy = {k: remote(g_mine, g_mine, 9 + k, plane_peer(k)) for k in flips}
    small_copy = {k: remote(small.at[me], small.at[me], 12 + k, plane_peer(k)) for k in flips}

    for load in loads[:4]:
        load.wait()
    angles = steps_v[y].astype(F32) * freqs_v[...]
    features = jnp.concatenate([jnp.cos(angles), jnp.sin(angles)], axis=1)
    parts = rows_of(*[p.astype(F32) for p in thirds(features)]).astype(BF16)
    embedded = jnp.dot(parts, emb_v[...], preferred_element_type=F32)
    embedded = embedded[0:1] + (embedded[1:2] + embedded[2:3])
    scales1 = 1.0 + embedded[:, :C]
    shifts = embedded[:, C:]
    gains = gain_v[...]
    factor = gains * scales1
    same = (
        lax.broadcasted_iota(jnp.int32, (C, C), 0) // (C // G)
        == lax.broadcasted_iota(jnp.int32, (C, C), 1) // (C // G)
    ).astype(F32).astype(BF16)
    cells = PIX * (C // G)

    clear_border(act_cols)
    for i in range(4):
        clear_border(g_cols.at[i])

    pl.semaphore_wait(barrier, len(partners))

    @pl.when(s == 0)
    def _():
        for k in (1, 2, 3):
            image_row(k).start()

    @pl.when(s == last)
    def _():
        for k in (1, 2, 3):
            grad_row(k).start()

    loads[4].wait()

    def turn_weights():
        for ky in range(3):
            for kx in range(3):
                turned[ky, kx * C : (kx + 1) * C, :] = plain[2 - ky, 2 - kx].T

    def back_convolve():
        spread_columns(g_cols_mine, g_mine[...].astype(F32))
        d_act[...] = convolve(g_cols_mine, turned[...])

    def share_grad():
        for k in flips:
            g_copy[k].start()

    @pl.when(s == 0)
    def _():
        own_image.start()
        own_image.wait()
        for k in (1, 2, 3):
            image_row(k).wait_recv()

    @pl.when(s == last)
    def _():
        own_grad.start()
        turn_weights()
        own_grad.wait()
        for k in (1, 2, 3):
            grad_row(k).wait_recv()
        back_convolve()

    @pl.when(s > 0)
    def _():
        forward_hop.wait_recv()

    @pl.when(s == last)
    def _():
        forward_skip.wait_recv()
        hbuf[...] = (hbuf[...].astype(F32) + skip[...].astype(F32)).astype(BF16)

    tensor = hbuf[...].astype(F32)
    first = jnp.sum(tensor, axis=0, keepdims=True)
    square = jnp.sum(tensor * tensor, axis=0, keepdims=True)
    average, mean_square = group_means(first, square, same, 1.0 / cells)
    inverse = lax.rsqrt(mean_square - average * average + EPS)
    normal = (tensor - average) * inverse
    normed[...] = normal
    pre = normal * factor + shifts
    sigmoid = jax.nn.sigmoid(pre)
    act = pre * sigmoid

    @pl.when(s < last)
    def _():
        spread_columns(act_cols, act)
        out = convolve(act_cols, plain[...])
        obuf[...] = (hbuf[...].astype(F32) + out).astype(BF16)
        forward_hop.start()

    @pl.when(s == 0)
    def _():
        forward_skip.start()

    slope[...] = sigmoid * (1.0 + pre * (1.0 - sigmoid))

    def share_act(value):
        act_t[me] = value.T
        for k in flips:
            act_copy[k].start()

    @pl.when(s < last)
    def _():
        share_act(act.astype(BF16))

    @pl.when(s == last)
    def _():
        obuf[...] = act.astype(BF16)

    @pl.when(s < last)
    def _():
        turn_weights()
        backward_hop.wait_recv()

    @pl.when(s == 0)
    def _():
        backward_skip.wait_recv()
        g_all[me] = (g_mine[...].astype(F32) + gskip[...].astype(F32)).astype(BF16)

    @pl.when(s == 0)
    def _():
        share_grad()

    @pl.when(s < last)
    def _():
        back_convolve()

    d_pre = d_act[...] * slope[...]
    normal = normed[...]
    sum_pre = jnp.sum(d_pre, axis=0, keepdims=True)
    sum_normal = jnp.sum(d_pre * normal, axis=0, keepdims=True)

    @pl.when(s > 0)
    def _():
        mean_d, mean_dn = group_means(sum_pre * factor, sum_normal * factor, same, 1.0 / cells)
        d_tensor = inverse * (d_pre * factor - mean_d - normal * mean_dn)
        dbuf[...] = (g_mine[...].astype(F32) + d_tensor).astype(BF16)
        backward_hop.start()
        share_grad()

    @pl.when(s == last)
    def _():
        backward_skip.start()
        share_act(obuf[...])

    small[me] = rows_of(sum_normal * gains, sum_pre, sum_normal * scales1, features)
    for k in flips:
        small_copy[k].start()

    def image_out(slot, number):
        return [
            pltpu.make_async_copy(act_t.at[slot], act_out.at[slot], leave.at[number]),
            pltpu.make_async_copy(g_cols.at[slot], cols_out.at[slot], leave.at[4 + number]),
        ]

    leaving = image_out(me, 0)
    for copy in leaving:
        copy.start()
    for k in flips:
        act_copy[k].wait_recv()
    for k in flips:
        g_copy[k].wait_recv()
        other = me ^ (((k & 1) << 1) | (k >> 1))
        spread_columns(g_cols.at[other], g_all[other].astype(F32))
        for copy in image_out(other, k):
            copy.start()
            leaving.append(copy)
    for k in flips:
        small_copy[k].wait_recv()
    leaving.append(pltpu.make_async_copy(small, small_out, leave.at[8]))
    leaving[-1].start()

    @pl.when(s == 0)
    def _():
        for k in (1, 2, 3):
            image_row(k).wait_send()
        forward_skip.wait_send()

    @pl.when(s == last)
    def _():
        for k in (1, 2, 3):
            grad_row(k).wait_send()
        backward_skip.wait_send()

    @pl.when(s < last)
    def _():
        forward_hop.wait_send()

    @pl.when(s > 0)
    def _():
        backward_hop.wait_send()

    for k in flips:
        act_copy[k].wait_send()
        g_copy[k].wait_send()
        small_copy[k].wait_send()
    for copy in leaving:
        copy.wait()


def grad_body(
    slots, act_in, cols_in, small_in, conv_out, gain_out, emb_out,
    act_t, g_cols, small, taps, gain_v, emb_v, sems,
):
    loads = [pltpu.make_async_copy(small_in, small, sems.at[11])]
    for i in range(slots):
        loads.append(pltpu.make_async_copy(act_in.at[i], act_t.at[i], sems.at[12 + i]))
        loads.append(pltpu.make_async_copy(cols_in.at[i], g_cols.at[i], sems.at[16 + i]))
    for load in loads:
        load.start()
    loads[0].wait()
    packed = [small[i] for i in range(slots)]
    gain_total = packed[0][2:3]
    for block in packed[1:]:
        gain_total = gain_total + block[2:3]
    gain_v[...] = gain_total
    features = rows_of(*[block[3:4] for block in packed])
    d_rows = rows_of(*[jnp.concatenate([block[0:1], block[1:2]], axis=1) for block in packed])
    emb_v[...] = jnp.dot(
        features.T, d_rows, precision=lax.Precision.HIGHEST, preferred_element_type=F32
    )
    copies = [
        pltpu.make_async_copy(gain_v, gain_out, sems.at[9]),
        pltpu.make_async_copy(emb_v, emb_out.at[0], sems.at[10]),
    ]
    for copy in copies:
        copy.start()
    for load in loads[1:]:
        load.wait()
    left = jnp.concatenate([act_t[i] for i in range(slots)], axis=1)
    for ky in range(3):
        for kx in range(3):
            rows, lanes = slice(ky * COLS, ky * COLS + PIX), slice(kx * C, (kx + 1) * C)
            right = jnp.concatenate([g_cols[i, rows, lanes] for i in range(slots)], axis=0)
            total = jnp.dot(left, right, preferred_element_type=F32)
            tap = ky * 3 + kx
            taps[tap] = total
            copy = pltpu.make_async_copy(taps.at[tap], conv_out.at[0, 2 - ky, 2 - kx], sems.at[tap])
            copy.start()
            copies.append(copy)
    for copy in copies:
        copy.wait()


def per_device(images, steps, out_grad, conv_weight, gn_gain, emb_weight):
    n_dp = lax.axis_size("dp")
    n_sec = lax.axis_size("section")
    flips = (1, 2, 3) if n_dp == 2 else (2,)
    half = C // 2
    freqs = np.exp(-math.log(10000.0) * np.arange(half, dtype=np.float32) / half)
    hbm = pl.BlockSpec(memory_space=pltpu.HBM)
    padded = PIX + 2 * COLS
    chain = pl.pallas_call(
        functools.partial(chain_body, n_sec, flips),
        out_shape=(
            jax.ShapeDtypeStruct((4, C, PIX), BF16),
            jax.ShapeDtypeStruct((4, padded, 3 * C), BF16),
            jax.ShapeDtypeStruct((4, 8, C), F32),
        ),
        in_specs=[hbm] * 7,
        out_specs=(hbm, hbm, hbm),
        scratch_shapes=[
            pltpu.VMEM((4, C, PIX), BF16),
            pltpu.VMEM((4, padded, 3 * C), BF16),
            pltpu.VMEM((4, 8, C), F32),
            pltpu.VMEM((PIX, C), BF16),
            pltpu.VMEM((PIX, C), BF16),
            pltpu.VMEM((PIX, C), BF16),
            pltpu.VMEM((PIX, C), BF16),
            pltpu.VMEM((PIX, C), BF16),
            pltpu.VMEM((4, PIX, C), BF16),
            pltpu.VMEM((3, 3, C, C), BF16),
            pltpu.VMEM((3, 3 * C, C), BF16),
            pltpu.VMEM((padded, 3 * C), BF16),
            pltpu.VMEM((PIX, C), F32),
            pltpu.VMEM((PIX, C), F32),
            pltpu.VMEM((PIX, C), F32),
            pltpu.SMEM((2,), jnp.int32),
            pltpu.VMEM((1, C // 2), F32),
            pltpu.VMEM((1, C), F32),
            pltpu.VMEM((C, 2 * C), BF16),
            pltpu.SemaphoreType.DMA((16,)),
            pltpu.SemaphoreType.DMA((16,)),
            pltpu.SemaphoreType.DMA((6,)),
            pltpu.SemaphoreType.DMA((9,)),
        ],
        compiler_params=pltpu.CompilerParams(
            collective_id=0, has_side_effects=True, vmem_limit_bytes=56 * 1024 * 1024
        ),
    )(
        steps, jnp.asarray(freqs, F32)[None, :], images, out_grad, conv_weight, gn_gain, emb_weight
    )
    grads = pl.pallas_call(
        functools.partial(grad_body, 4 if n_dp == 2 else 2),
        out_shape=(
            jax.ShapeDtypeStruct((1, 3, 3, C, C), F32),
            jax.ShapeDtypeStruct((1, C), F32),
            jax.ShapeDtypeStruct((1, C, 2 * C), F32),
        ),
        in_specs=[hbm] * 3,
        out_specs=(hbm, hbm, hbm),
        scratch_shapes=[
            pltpu.VMEM((4, C, PIX), BF16),
            pltpu.VMEM((4, padded, 3 * C), BF16),
            pltpu.VMEM((4, 8, C), F32),
            pltpu.VMEM((9, C, C), F32),
            pltpu.VMEM((1, C), F32),
            pltpu.VMEM((C, 2 * C), F32),
            pltpu.SemaphoreType.DMA((20,)),
        ],
        compiler_params=pltpu.CompilerParams(vmem_limit_bytes=56 * 1024 * 1024),
    )(*chain)
    if n_dp != 2:
        grads = lax.psum(grads, "dp")
    return grads


def solution(mesh):
    in_specs = (
        P("dp", "space", None, None),
        P("dp"),
        P("dp", "space", None, None),
        P("section", None, None, None, None),
        P("section", None),
        P("section", None, None),
    )
    out_specs = (P("section", None, None, None, None), P("section", None), P("section", None, None))
    return jax.shard_map(
        per_device, mesh=mesh, in_specs=in_specs, out_specs=out_specs, check_vma=False
    )
```

```python
import functools
import math

import jax
import jax.numpy as jnp
import numpy as np
from jax import lax
from jax.experimental import pallas as pl
from jax.experimental.pallas import tpu as pltpu
from jax.sharding import PartitionSpec as P

G = 32
EPS = 1e-05
MESH = pl.DeviceIdType.MESH
F32 = jnp.float32
BF16 = jnp.bfloat16
PIX = 256
COLS = 64
C = 256
HALF = 128


def thirds(x):
    first = x.astype(BF16)
    rest = x - first.astype(F32)
    second = rest.astype(BF16)
    return first, second, (rest - second.astype(F32)).astype(BF16)


def rows_of(*rows):
    index = lax.broadcasted_iota(jnp.int32, (8, rows[0].shape[1]), 0)
    out = jnp.zeros((8, rows[0].shape[1]), F32)
    for i, row in enumerate(rows):
        out = jnp.where(index == i, row, out)
    return out


def half_at(index):
    return pl.ds(pl.multiple_of(index * HALF, HALF), HALF)


def group_means(first, second, same, scale):
    parts = [p.astype(F32) for p in thirds(first) + thirds(second)]
    sums = jnp.dot(rows_of(*parts).astype(BF16), same, preferred_element_type=F32) * scale
    return sums[0:1] + (sums[1:2] + sums[2:3]), sums[3:4] + (sums[4:5] + sums[5:6])


def spread_columns(ref, value, half):
    column = lax.broadcasted_iota(jnp.int32, (PIX, HALF), 0) & (COLS - 1)
    left = jnp.where(column == 0, 0.0, pltpu.roll(value, 1, 0))
    right = jnp.where(column == COLS - 1, 0.0, pltpu.roll(value, PIX - 1, 0))
    for kx, moved in enumerate((left, value, right)):
        ref[COLS : COLS + PIX, half_at(2 * kx + half)] = moved.astype(BF16)


def clear_border(ref):
    blank = jnp.zeros((COLS, 3 * C), BF16)
    ref[0:COLS, :] = blank
    ref[COLS + PIX : 2 * COLS + PIX, :] = blank


def convolve(ref, kernel, half):
    left = jnp.concatenate(
        [
            ref[ky * COLS : ky * COLS + PIX, half_at(2 * kx + half)]
            for ky in range(3)
            for kx in range(3)
        ],
        axis=1,
    )
    right = kernel[:, :, half_at(half), :].reshape(9 * HALF, HALF)
    return jnp.dot(left, right, preferred_element_type=F32)


def chain_body(
    n_sec, flips, steps, freqs, images, out_grad, weight, gain, emb,
    act_out, cols_out, small_out,
    act_t, g_cols, small, hbuf, skip, gskip, obuf, dbuf, act_raw, g_all, plain, across, turned, act_cols,
    normed, slope, d_act, steps_v, freqs_v, gain_v, emb_v, send, recv, local, leave, ready,
):
    dp = lax.axis_index("dp")
    s = lax.axis_index("section")
    space = lax.axis_index("space")
    y = space // 2
    core = lax.rem(space, 2)
    last = n_sec - 1
    me = dp * 2 + y if len(flips) == 3 else y
    ahead, behind = lax.rem(s + 1, n_sec), lax.rem(s + n_sec - 1, n_sec)
    sibling = {"space": space ^ 1}

    def plane_peer(k, flip_core=0):
        return {"dp": dp ^ (k & 1), "space": space ^ (k & 2) ^ flip_core}

    others = [(k, f) for k in (0,) + flips for f in (0, 1) if k or f]
    barrier = pltpu.get_barrier_semaphore()
    partners = [plane_peer(k, f) if k & 1 else {"space": space ^ (k & 2) ^ f} for k, f in others]
    for partner in partners:
        pl.semaphore_signal(barrier, inc=1, device_id=partner, device_id_type=MESH)
    for partner in (ahead, behind):

        @pl.when(partner != 0)
        def _():
            pl.semaphore_signal(
                barrier, inc=1, device_id={"section": partner}, device_id_type=MESH
            )

    loads = [
        pltpu.make_async_copy(src, dst, local.at[i])
        for i, (src, dst) in enumerate((
            (steps, steps_v),
            (freqs, freqs_v),
            (emb.at[0, :, half_at(core)], emb_v.at[0]),
            (emb.at[0, :, half_at(core + 2)], emb_v.at[1]),
            (gain.at[:, half_at(core)], gain_v),
            (weight.at[0, :, :, :, half_at(core)], plain),
            (weight.at[0, :, :, half_at(core), :], across),
        ))
    ]
    for load in loads:
        load.start()

    def remote(src, dst, number, device):
        return pltpu.make_async_remote_copy(
            src_ref=src, dst_ref=dst, send_sem=send.at[number], recv_sem=recv.at[number],
            device_id=device, device_id_type=MESH,
        )

    def row_at(index):
        return pl.ds(pl.multiple_of(index * COLS, COLS), COLS)

    g_mine = g_all.at[me, core]
    g_cols_mine = g_cols.at[me]
    act_rows = half_at(core)

    def image_row(k):
        target = space ^ k
        return remote(
            images.at[target // 2, 0, :, half_at(lax.rem(target, 2))],
            hbuf.at[row_at(space), :], k - 1, {"space": target},
        )

    def grad_row(k):
        target = space ^ k
        return remote(
            out_grad.at[target // 2, 0, :, half_at(lax.rem(target, 2))],
            g_all.at[me ^ (k >> 1), lax.rem(target, 2), row_at(space), :],
            k - 1, {"space": target},
        )

    own_image = pltpu.make_async_copy(
        images.at[y, 0, :, half_at(core)], hbuf.at[row_at(space), :], local.at[7]
    )
    own_grad = pltpu.make_async_copy(
        out_grad.at[y, 0, :, half_at(core)], g_all.at[me, core, row_at(space), :], local.at[7]
    )
    forward_hop = remote(obuf, hbuf, 3, {"section": ahead})
    forward_skip = remote(obuf, skip, 4, {"section": behind})
    backward_hop = remote(dbuf, g_mine, 5, {"section": behind})
    backward_skip = remote(dbuf, gskip, 6, {"section": ahead})
    act_sibling = remote(act_raw.at[core], act_raw.at[core], 7, sibling)
    g_sibling = remote(g_mine, g_mine, 8, sibling)
    act_copy, g_copy, act_pass, g_pass, slot = {}, {}, {}, {}, {}
    for k in flips:
        slot[k] = me ^ (((k & 1) << 1) | (k >> 1))
        mine = act_t.at[me, act_rows, :]
        theirs = act_t.at[slot[k], act_rows, :]
        act_copy[k] = remote(mine, mine, 8 + k, plane_peer(k))
        g_copy[k] = remote(g_mine, g_mine, 11 + k, plane_peer(k))
        act_pass[k] = remote(theirs, theirs, 14 + k, sibling)
        passed = g_all.at[slot[k], core]
        g_pass[k] = remote(passed, passed, 17 + k, sibling)
    small_copy = [
        remote(small.at[me, core], small.at[me, core], 21 + i, plane_peer(k, f))
        for i, (k, f) in enumerate(others)
    ]

    for load in loads[:5]:
        load.wait()
    angles = steps_v[y].astype(F32) * freqs_v[...]
    cosines, sines = jnp.cos(angles), jnp.sin(angles)
    features = jnp.concatenate([cosines, sines], axis=1)
    features = rows_of(*[p.astype(F32) for p in thirds(features)]).astype(BF16)
    scales1, shifts = (
        part[0:1] + (part[1:2] + part[2:3])
        for part in (
            jnp.dot(features, emb_v[i], preferred_element_type=F32) for i in range(2)
        )
    )
    scales1 = 1.0 + scales1
    gains = gain_v[...]
    factor = gains * scales1

    clear_border(act_cols)
    for i in range(4):
        clear_border(g_cols.at[i])
    same = (
        lax.broadcasted_iota(jnp.int32, (HALF, HALF), 0) // (C // G)
        == lax.broadcasted_iota(jnp.int32, (HALF, HALF), 1) // (C // G)
    ).astype(F32).astype(BF16)
    cells = PIX * (C // G)

    @pl.when(s == 0)
    def _():
        pl.semaphore_wait(barrier, len(partners))

    @pl.when(s > 0)
    def _():
        pl.semaphore_wait(barrier, len(partners) + 2)

    @pl.when((ahead == 0) | (behind == 0))
    def _():
        pl.semaphore_signal(ready, inc=1, device_id={"section": 0}, device_id_type=MESH)

    @pl.when(s == 0)
    def _():
        for k in (1, 2, 3):
            image_row(k).start()
        own_image.start()

    @pl.when(s == last)
    def _():
        for k in (1, 2, 3):
            grad_row(k).start()
        own_grad.start()

    for load in loads[5:]:
        load.wait()

    def turn_weights():
        for ky in range(3):
            for kx in range(3):
                turned[ky, kx] = across[2 - ky, 2 - kx].T

    def back_convolve():
        g_sibling.start()
        spread_columns(g_cols_mine, g_mine[...].astype(F32), core)
        total = convolve(g_cols_mine, turned, core)
        g_sibling.wait_recv()
        spread_columns(g_cols_mine, g_all[me, 1 - core].astype(F32), 1 - core)
        d_act[...] = total + convolve(g_cols_mine, turned, 1 - core)

    @pl.when(s == 0)
    def _():
        own_image.wait()
        for k in (1, 2, 3):
            image_row(k).wait_recv()

    @pl.when(s == last)
    def _():
        turn_weights()
        own_grad.wait()
        for k in (1, 2, 3):
            grad_row(k).wait_recv()
        back_convolve()

    @pl.when(s > 0)
    def _():
        forward_hop.wait_recv()

    @pl.when(s == last)
    def _():
        forward_skip.wait_recv()
        hbuf[...] = (hbuf[...].astype(F32) + skip[...].astype(F32)).astype(BF16)

    tensor = hbuf[...].astype(F32)
    first = jnp.sum(tensor, axis=0, keepdims=True)
    square = jnp.sum(tensor * tensor, axis=0, keepdims=True)
    average, mean_square = group_means(first, square, same, 1.0 / cells)
    inverse = lax.rsqrt(mean_square - average * average + EPS)
    normal = (tensor - average) * inverse
    normed[...] = normal
    pre = normal * factor + shifts
    sigmoid = jax.nn.sigmoid(pre)
    act = pre * sigmoid
    act_raw[core] = act.astype(BF16)
    act_sibling.start()

    @pl.when(s < last)
    def _():
        spread_columns(act_cols, act, core)
        out = hbuf[...].astype(F32) + convolve(act_cols, plain, core)
        act_sibling.wait_recv()
        spread_columns(act_cols, act_raw[1 - core].astype(F32), 1 - core)
        obuf[...] = (out + convolve(act_cols, plain, 1 - core)).astype(BF16)

        @pl.when(s == 0)
        def _():
            pl.semaphore_wait(ready, 2)

        forward_hop.start()

    slope[...] = sigmoid * (1.0 + pre * (1.0 - sigmoid))

    def share_act():
        act_t[me, act_rows, :] = act_raw[core].T
        for k in flips:
            act_copy[k].start()
        act_t[me, half_at(1 - core), :] = act_raw[1 - core].T

    @pl.when(s < last)
    def _():
        share_act()
        turn_weights()
        forward_hop.wait_send()

    @pl.when(s == 0)
    def _():
        forward_skip.start()

    @pl.when(s < last)
    def _():
        backward_hop.wait_recv()

    @pl.when(s == 0)
    def _():
        backward_skip.wait_recv()
        g_all[me, core] = (g_mine[...].astype(F32) + gskip[...].astype(F32)).astype(BF16)

    def share_grad():
        for k in reversed(flips):
            g_copy[k].start()

    @pl.when(s == 0)
    def _():
        share_grad()

    @pl.when(s < last)
    def _():
        back_convolve()

    d_pre = d_act[...] * slope[...]
    normal = normed[...]
    sum_pre = jnp.sum(d_pre, axis=0, keepdims=True)
    sum_normal = jnp.sum(d_pre * normal, axis=0, keepdims=True)

    @pl.when(s > 0)
    def _():
        mean_d, mean_dn = group_means(sum_pre * factor, sum_normal * factor, same, 1.0 / cells)
        d_tensor = inverse * (d_pre * factor - mean_d - normal * mean_dn)
        dbuf[...] = (g_mine[...].astype(F32) + d_tensor).astype(BF16)
        backward_hop.start()
        share_grad()

    @pl.when(s == last)
    def _():
        act_sibling.wait_recv()
        share_act()
        backward_hop.wait_send()
        backward_skip.start()

    small[me, core] = rows_of(sum_normal * gains, sum_pre, sum_normal * scales1, cosines, sines)
    for copy in small_copy:
        copy.start()

    def image_out(slot_no, number):
        return [
            pltpu.make_async_copy(act_t.at[slot_no], act_out.at[slot_no], leave.at[number]),
            pltpu.make_async_copy(g_cols.at[slot_no], cols_out.at[slot_no], leave.at[4 + number]),
        ]

    leaving = image_out(me, 0)
    for copy in leaving:
        copy.start()

    for k in flips:
        act_copy[k].wait_recv()
        act_pass[k].start()
    for k in flips:
        g_copy[k].wait_recv()
        g_pass[k].start()
        spread_columns(g_cols.at[slot[k]], g_all[slot[k], core].astype(F32), core)
    for k in flips:
        act_pass[k].wait_recv()
        g_pass[k].wait_recv()
        spread_columns(g_cols.at[slot[k]], g_all[slot[k], 1 - core].astype(F32), 1 - core)
        for copy in image_out(slot[k], k):
            copy.start()
            leaving.append(copy)
    for copy in small_copy:
        copy.wait_recv()
    leaving.append(pltpu.make_async_copy(small, small_out, leave.at[8]))
    leaving[-1].start()

    @pl.when(s == 0)
    def _():
        for k in (1, 2, 3):
            image_row(k).wait_send()
        forward_skip.wait_send()

    @pl.when(s == last)
    def _():
        for k in (1, 2, 3):
            grad_row(k).wait_send()
        backward_skip.wait_send()

    @pl.when((s > 0) & (s < last))
    def _():
        backward_hop.wait_send()

    act_sibling.wait_send()
    g_sibling.wait_send()
    for k in flips:
        for copy in (act_copy[k], g_copy[k], act_pass[k], g_pass[k]):
            copy.wait_send()
    for copy in small_copy:
        copy.wait_send()
    for copy in leaving:
        copy.wait()


def grad_body(
    slots, act_in, cols_in, small_in, conv_out, gain_out, emb_out,
    act_t, g_cols, small, taps, gain_v, emb_v, sems,
):
    loads = [pltpu.make_async_copy(small_in, small, sems.at[11])]
    for i in range(slots):
        loads.append(pltpu.make_async_copy(act_in.at[i], act_t.at[i], sems.at[12 + i]))
        loads.append(pltpu.make_async_copy(cols_in.at[i], g_cols.at[i], sems.at[16 + i]))
    for load in loads:
        load.start()
    loads[0].wait()
    packed = [jnp.concatenate([small[i, 0], small[i, 1]], axis=1) for i in range(slots)]
    gain_total = packed[0][2:3]
    for block in packed[1:]:
        gain_total = gain_total + block[2:3]
    gain_v[...] = gain_total
    features = rows_of(
        *[jnp.concatenate([small[i, 0, 3:4], small[i, 0, 4:5]], axis=1) for i in range(slots)]
    )
    d_rows = rows_of(*[jnp.concatenate([block[0:1], block[1:2]], axis=1) for block in packed])
    emb_v[...] = jnp.dot(
        features.T, d_rows, precision=lax.Precision.HIGHEST, preferred_element_type=F32
    )
    copies = [
        pltpu.make_async_copy(gain_v, gain_out, sems.at[9]),
        pltpu.make_async_copy(emb_v, emb_out.at[0], sems.at[10]),
    ]
    for copy in copies:
        copy.start()
    for load in loads[1:]:
        load.wait()
    left = jnp.concatenate([act_t[i] for i in range(slots)], axis=1)
    for ky in range(3):
        for kx in range(3):
            rows, lanes = slice(ky * COLS, ky * COLS + PIX), slice(kx * C, (kx + 1) * C)
            right = jnp.concatenate([g_cols[i, rows, lanes] for i in range(slots)], axis=0)
            total = jnp.dot(left, right, preferred_element_type=F32)
            tap = ky * 3 + kx
            taps[tap] = total
            copy = pltpu.make_async_copy(taps.at[tap], conv_out.at[0, 2 - ky, 2 - kx], sems.at[tap])
            copy.start()
            copies.append(copy)
    for copy in copies:
        copy.wait()


def per_device(images, steps, out_grad, conv_weight, gn_gain, emb_weight):
    n_dp = lax.axis_size("dp")
    n_sec = lax.axis_size("section")
    flips = (1, 2, 3) if n_dp == 2 else (2,)
    half = C // 2
    freqs = np.exp(-math.log(10000.0) * np.arange(half, dtype=np.float32) / half)
    hbm = pl.BlockSpec(memory_space=pltpu.HBM)
    padded = PIX + 2 * COLS
    chain = pl.pallas_call(
        functools.partial(chain_body, n_sec, flips),
        out_shape=(
            jax.ShapeDtypeStruct((4, C, PIX), BF16),
            jax.ShapeDtypeStruct((4, padded, 3 * C), BF16),
            jax.ShapeDtypeStruct((4, 2, 8, HALF), F32),
        ),
        in_specs=[hbm] * 7,
        out_specs=(hbm, hbm, hbm),
        scratch_shapes=[
            pltpu.VMEM((4, C, PIX), BF16),
            pltpu.VMEM((4, padded, 3 * C), BF16),
            pltpu.VMEM((4, 2, 8, HALF), F32),
            pltpu.VMEM((PIX, HALF), BF16),
            pltpu.VMEM((PIX, HALF), BF16),
            pltpu.VMEM((PIX, HALF), BF16),
            pltpu.VMEM((PIX, HALF), BF16),
            pltpu.VMEM((PIX, HALF), BF16),
            pltpu.VMEM((2, PIX, HALF), BF16),
            pltpu.VMEM((4, 2, PIX, HALF), BF16),
            pltpu.VMEM((3, 3, C, HALF), BF16),
            pltpu.VMEM((3, 3, HALF, C), BF16),
            pltpu.VMEM((3, 3, C, HALF), BF16),
            pltpu.VMEM((padded, 3 * C), BF16),
            pltpu.VMEM((PIX, HALF), F32),
            pltpu.VMEM((PIX, HALF), F32),
            pltpu.VMEM((PIX, HALF), F32),
            pltpu.SMEM((2,), jnp.int32),
            pltpu.VMEM((1, HALF), F32),
            pltpu.VMEM((1, HALF), F32),
            pltpu.VMEM((2, C, HALF), BF16),
            pltpu.SemaphoreType.DMA((28,)),
            pltpu.SemaphoreType.DMA((28,)),
            pltpu.SemaphoreType.DMA((8,)),
            pltpu.SemaphoreType.DMA((9,)),
            pltpu.SemaphoreType.REGULAR,
        ],
        compiler_params=pltpu.CompilerParams(
            collective_id=0, has_side_effects=True, vmem_limit_bytes=56 * 1024 * 1024
        ),
    )(
        steps, jnp.asarray(freqs, F32)[None, :], images, out_grad, conv_weight, gn_gain, emb_weight
    )
    grads = pl.pallas_call(
        functools.partial(grad_body, 4 if n_dp == 2 else 2),
        out_shape=(
            jax.ShapeDtypeStruct((1, 3, 3, C, C), F32),
            jax.ShapeDtypeStruct((1, C), F32),
            jax.ShapeDtypeStruct((1, C, 2 * C), F32),
        ),
        in_specs=[hbm] * 3,
        out_specs=(hbm, hbm, hbm),
        scratch_shapes=[
            pltpu.VMEM((4, C, PIX), BF16),
            pltpu.VMEM((4, padded, 3 * C), BF16),
            pltpu.VMEM((4, 2, 8, HALF), F32),
            pltpu.VMEM((9, C, C), F32),
            pltpu.VMEM((1, C), F32),
            pltpu.VMEM((C, 2 * C), F32),
            pltpu.SemaphoreType.DMA((20,)),
        ],
        compiler_params=pltpu.CompilerParams(vmem_limit_bytes=56 * 1024 * 1024),
    )(*chain)
    if n_dp != 2:
        grads = lax.psum(grads, "dp")
    return grads


def solution(mesh):
    in_specs = (
        P("dp", "space", None, None),
        P("dp"),
        P("dp", "space", None, None),
        P("section", None, None, None, None),
        P("section", None),
        P("section", None, None),
    )
    out_specs = (P("section", None, None, None, None), P("section", None), P("section", None, None))
    return jax.shard_map(
        per_device, mesh=mesh, in_specs=in_specs, out_specs=out_specs, check_vma=False
    )
```

```python
import functools
import math

import jax
import jax.numpy as jnp
import numpy as np
from jax import lax
from jax.experimental import pallas as pl
from jax.experimental.pallas import tpu as pltpu
from jax.sharding import PartitionSpec as P

G = 32
EPS = 1e-05
MESH = pl.DeviceIdType.MESH
F32 = jnp.float32
BF16 = jnp.bfloat16
PIX = 256
COLS = 64
C = 256
HALF = 128


def thirds(x):
    first = x.astype(BF16)
    rest = x - first.astype(F32)
    second = rest.astype(BF16)
    return first, second, (rest - second.astype(F32)).astype(BF16)


def rows_of(*rows):
    index = lax.broadcasted_iota(jnp.int32, (8, rows[0].shape[1]), 0)
    out = jnp.zeros((8, rows[0].shape[1]), F32)
    for i, row in enumerate(rows):
        out = jnp.where(index == i, row, out)
    return out


def half_at(index):
    return pl.ds(pl.multiple_of(index * HALF, HALF), HALF)


def group_means(first, second, same, scale):
    parts = [p.astype(F32) for p in thirds(first) + thirds(second)]
    sums = jnp.dot(rows_of(*parts).astype(BF16), same, preferred_element_type=F32) * scale
    return sums[0:1] + (sums[1:2] + sums[2:3]), sums[3:4] + (sums[4:5] + sums[5:6])


def spread_columns(ref, value, half):
    column = lax.broadcasted_iota(jnp.int32, (PIX, HALF), 0) & (COLS - 1)
    left = jnp.where(column == 0, 0.0, pltpu.roll(value, 1, 0))
    right = jnp.where(column == COLS - 1, 0.0, pltpu.roll(value, PIX - 1, 0))
    for kx, moved in enumerate((left, value, right)):
        ref[COLS : COLS + PIX, half_at(2 * kx + half)] = moved.astype(BF16)


def clear_border(ref):
    blank = jnp.zeros((COLS, 3 * C), BF16)
    ref[0:COLS, :] = blank
    ref[COLS + PIX : 2 * COLS + PIX, :] = blank


def convolve(ref, kernel, half):
    left = jnp.concatenate(
        [
            ref[ky * COLS : ky * COLS + PIX, half_at(2 * kx + half)]
            for ky in range(3)
            for kx in range(3)
        ],
        axis=1,
    )
    right = kernel[:, :, half_at(half), :].reshape(9 * HALF, HALF)
    return jnp.dot(left, right, preferred_element_type=F32)


def chain_body(
    n_sec, flips, steps, freqs, images, out_grad, weight, gain, emb,
    act_out, cols_out, small_out,
    act_t, g_cols, small, hbuf, skip, gskip, obuf, dbuf, act_raw, g_all, plain, across, turned, act_cols,
    normed, slope, d_act, steps_v, freqs_v, gain_v, emb_v, send, recv, local, leave, ready,
):
    dp = lax.axis_index("dp")
    s = lax.axis_index("section")
    space = lax.axis_index("space")
    y = space // 2
    core = lax.rem(space, 2)
    last = n_sec - 1
    me = dp * 2 + y if len(flips) == 3 else y
    ahead, behind = lax.rem(s + 1, n_sec), lax.rem(s + n_sec - 1, n_sec)
    sibling = {"space": space ^ 1}

    def plane_peer(k, flip_core=0):
        return {"dp": dp ^ (k & 1), "space": space ^ (k & 2) ^ flip_core}

    others = [(k, f) for k in (0,) + flips for f in (0, 1) if k or f]
    barrier = pltpu.get_barrier_semaphore()
    partners = [plane_peer(k, f) if k & 1 else {"space": space ^ (k & 2) ^ f} for k, f in others]
    for partner in partners:
        pl.semaphore_signal(barrier, inc=1, device_id=partner, device_id_type=MESH)
    for partner in (ahead, behind):

        @pl.when(partner != 0)
        def _():
            pl.semaphore_signal(
                barrier, inc=1, device_id={"section": partner}, device_id_type=MESH
            )

    loads = [
        pltpu.make_async_copy(src, dst, local.at[i])
        for i, (src, dst) in enumerate((
            (steps, steps_v),
            (freqs, freqs_v),
            (emb.at[0, :, half_at(core)], emb_v.at[0]),
            (emb.at[0, :, half_at(core + 2)], emb_v.at[1]),
            (gain.at[:, half_at(core)], gain_v),
            (weight.at[0, :, :, :, half_at(core)], plain),
            (weight.at[0, :, :, half_at(core), :], across),
        ))
    ]
    for load in loads:
        load.start()

    def remote(src, dst, number, device):
        return pltpu.make_async_remote_copy(
            src_ref=src, dst_ref=dst, send_sem=send.at[number], recv_sem=recv.at[number],
            device_id=device, device_id_type=MESH,
        )

    def row_at(index):
        return pl.ds(pl.multiple_of(index * COLS, COLS), COLS)

    g_mine = g_all.at[me, core]
    g_cols_mine = g_cols.at[me]
    act_rows = half_at(core)

    def image_row(k):
        target = space ^ k
        return remote(
            images.at[target // 2, 0, :, half_at(lax.rem(target, 2))],
            hbuf.at[row_at(space), :], k - 1, {"space": target},
        )

    def grad_row(k):
        target = space ^ k
        return remote(
            out_grad.at[target // 2, 0, :, half_at(lax.rem(target, 2))],
            g_all.at[me ^ (k >> 1), lax.rem(target, 2), row_at(space), :],
            k - 1, {"space": target},
        )

    own_image = pltpu.make_async_copy(
        images.at[y, 0, :, half_at(core)], hbuf.at[row_at(space), :], local.at[7]
    )
    own_grad = pltpu.make_async_copy(
        out_grad.at[y, 0, :, half_at(core)], g_all.at[me, core, row_at(space), :], local.at[7]
    )
    forward_hop = remote(obuf, hbuf, 3, {"section": ahead})
    forward_skip = remote(obuf, skip, 4, {"section": behind})
    backward_hop = remote(dbuf, g_mine, 5, {"section": behind})
    backward_skip = remote(dbuf, gskip, 6, {"section": ahead})
    act_sibling = remote(act_raw.at[core], act_raw.at[core], 7, sibling)
    g_sibling = remote(g_mine, g_mine, 8, sibling)
    act_copy, g_copy, act_pass, g_pass, slot = {}, {}, {}, {}, {}
    for k in flips:
        slot[k] = me ^ (((k & 1) << 1) | (k >> 1))
        mine = act_t.at[me, act_rows, :]
        theirs = act_t.at[slot[k], act_rows, :]
        act_copy[k] = remote(mine, mine, 8 + k, plane_peer(k))
        g_copy[k] = remote(g_mine, g_mine, 11 + k, plane_peer(k))
        act_pass[k] = remote(theirs, theirs, 14 + k, sibling)
        passed = g_all.at[slot[k], core]
        g_pass[k] = remote(passed, passed, 17 + k, sibling)
    small_copy = [
        remote(small.at[me, core], small.at[me, core], 21 + i, plane_peer(k, f))
        for i, (k, f) in enumerate(others)
    ]

    for load in loads[:5]:
        load.wait()
    angles = steps_v[y].astype(F32) * freqs_v[...]
    cosines, sines = jnp.cos(angles), jnp.sin(angles)
    features = jnp.concatenate([cosines, sines], axis=1)
    features = rows_of(*[p.astype(F32) for p in thirds(features)]).astype(BF16)
    scales1, shifts = (
        part[0:1] + (part[1:2] + part[2:3])
        for part in (
            jnp.dot(features, emb_v[i], preferred_element_type=F32) for i in range(2)
        )
    )
    scales1 = 1.0 + scales1
    gains = gain_v[...]
    factor = gains * scales1

    clear_border(act_cols)
    for i in range(4):
        clear_border(g_cols.at[i])
    same = (
        lax.broadcasted_iota(jnp.int32, (HALF, HALF), 0) // (C // G)
        == lax.broadcasted_iota(jnp.int32, (HALF, HALF), 1) // (C // G)
    ).astype(F32).astype(BF16)
    cells = PIX * (C // G)

    @pl.when(s == 0)
    def _():
        pl.semaphore_wait(barrier, len(partners))

    @pl.when(s > 0)
    def _():
        pl.semaphore_wait(barrier, len(partners) + 2)

    @pl.when((ahead == 0) | (behind == 0))
    def _():
        pl.semaphore_signal(ready, inc=1, device_id={"section": 0}, device_id_type=MESH)

    @pl.when(s == 0)
    def _():
        for k in (1, 2, 3):
            image_row(k).start()
        own_image.start()

    @pl.when(s == last)
    def _():
        for k in (1, 2, 3):
            grad_row(k).start()
        own_grad.start()

    for load in loads[5:]:
        load.wait()

    def turn_weights():
        for ky in range(3):
            for kx in range(3):
                turned[ky, kx] = across[2 - ky, 2 - kx].T

    def back_convolve():
        g_sibling.start()
        spread_columns(g_cols_mine, g_mine[...].astype(F32), core)
        total = convolve(g_cols_mine, turned, core)
        g_sibling.wait_recv()
        spread_columns(g_cols_mine, g_all[me, 1 - core].astype(F32), 1 - core)
        d_act[...] = total + convolve(g_cols_mine, turned, 1 - core)

    @pl.when(s == 0)
    def _():
        own_image.wait()
        for k in (1, 2, 3):
            image_row(k).wait_recv()

    @pl.when(s == last)
    def _():
        turn_weights()
        own_grad.wait()
        for k in (1, 2, 3):
            grad_row(k).wait_recv()
        back_convolve()

    @pl.when(s > 0)
    def _():
        forward_hop.wait_recv()

    @pl.when(s == last)
    def _():
        forward_skip.wait_recv()
        hbuf[...] = (hbuf[...].astype(F32) + skip[...].astype(F32)).astype(BF16)

    tensor = hbuf[...].astype(F32)
    first = jnp.sum(tensor, axis=0, keepdims=True)
    square = jnp.sum(tensor * tensor, axis=0, keepdims=True)
    average, mean_square = group_means(first, square, same, 1.0 / cells)
    inverse = lax.rsqrt(mean_square - average * average + EPS)
    normal = (tensor - average) * inverse
    normed[...] = normal
    pre = normal * factor + shifts
    sigmoid = jax.nn.sigmoid(pre)
    act = pre * sigmoid
    act_raw[core] = act.astype(BF16)
    act_sibling.start()

    @pl.when(s < last)
    def _():
        spread_columns(act_cols, act, core)
        out = hbuf[...].astype(F32) + convolve(act_cols, plain, core)
        act_sibling.wait_recv()
        spread_columns(act_cols, act_raw[1 - core].astype(F32), 1 - core)
        obuf[...] = (out + convolve(act_cols, plain, 1 - core)).astype(BF16)

        @pl.when(s == 0)
        def _():
            pl.semaphore_wait(ready, 2)

        forward_hop.start()

    slope[...] = sigmoid * (1.0 + pre * (1.0 - sigmoid))

    def share_act():
        act_t[me, act_rows, :] = act_raw[core].T
        for k in flips:
            act_copy[k].start()
        act_t[me, half_at(1 - core), :] = act_raw[1 - core].T

    def pass_act():
        for k in flips:
            act_copy[k].wait_recv()
            act_pass[k].start()

    @pl.when(s < last)
    def _():
        share_act()
        turn_weights()
        forward_hop.wait_send()

    @pl.when(s == 0)
    def _():
        forward_skip.start()

    @pl.when(s < last)
    def _():
        pass_act()
        backward_hop.wait_recv()

    @pl.when(s == 0)
    def _():
        backward_skip.wait_recv()
        g_all[me, core] = (g_mine[...].astype(F32) + gskip[...].astype(F32)).astype(BF16)

    def share_grad():
        for k in reversed(flips):
            g_copy[k].start()

    @pl.when(s == 0)
    def _():
        share_grad()

    @pl.when(s < last)
    def _():
        back_convolve()

    d_pre = d_act[...] * slope[...]
    normal = normed[...]
    sum_pre = jnp.sum(d_pre, axis=0, keepdims=True)
    sum_normal = jnp.sum(d_pre * normal, axis=0, keepdims=True)

    @pl.when(s > 0)
    def _():
        mean_d, mean_dn = group_means(sum_pre * factor, sum_normal * factor, same, 1.0 / cells)
        d_tensor = inverse * (d_pre * factor - mean_d - normal * mean_dn)
        dbuf[...] = (g_mine[...].astype(F32) + d_tensor).astype(BF16)
        backward_hop.start()
        share_grad()

    @pl.when(s == last)
    def _():
        act_sibling.wait_recv()
        share_act()
        backward_hop.wait_send()
        backward_skip.start()

    small[me, core] = rows_of(sum_normal * gains, sum_pre, sum_normal * scales1, cosines, sines)
    for copy in small_copy:
        copy.start()

    def image_out(slot_no, number):
        return [
            pltpu.make_async_copy(act_t.at[slot_no], act_out.at[slot_no], leave.at[number]),
            pltpu.make_async_copy(g_cols.at[slot_no], cols_out.at[slot_no], leave.at[4 + number]),
        ]

    leaving = image_out(me, 0)
    for copy in leaving:
        copy.start()

    @pl.when(s == last)
    def _():
        pass_act()

    for k in flips:
        g_copy[k].wait_recv()
        g_pass[k].start()
        spread_columns(g_cols.at[slot[k]], g_all[slot[k], core].astype(F32), core)
    for k in flips:
        act_pass[k].wait_recv()
        g_pass[k].wait_recv()
        spread_columns(g_cols.at[slot[k]], g_all[slot[k], 1 - core].astype(F32), 1 - core)
        for copy in image_out(slot[k], k):
            copy.start()
            leaving.append(copy)
    for copy in small_copy:
        copy.wait_recv()
    leaving.append(pltpu.make_async_copy(small, small_out, leave.at[8]))
    leaving[-1].start()

    @pl.when(s == 0)
    def _():
        for k in (1, 2, 3):
            image_row(k).wait_send()
        forward_skip.wait_send()

    @pl.when(s == last)
    def _():
        for k in (1, 2, 3):
            grad_row(k).wait_send()
        backward_skip.wait_send()

    @pl.when((s > 0) & (s < last))
    def _():
        backward_hop.wait_send()

    act_sibling.wait_send()
    g_sibling.wait_send()
    for k in flips:
        for copy in (act_copy[k], g_copy[k], act_pass[k], g_pass[k]):
            copy.wait_send()
    for copy in small_copy:
        copy.wait_send()
    for copy in leaving:
        copy.wait()


def grad_body(
    slots, act_in, cols_in, small_in, conv_out, gain_out, emb_out,
    act_t, g_cols, small, taps, gain_v, emb_v, sems,
):
    loads = [pltpu.make_async_copy(small_in, small, sems.at[11])]
    for i in range(slots):
        loads.append(pltpu.make_async_copy(act_in.at[i], act_t.at[i], sems.at[12 + i]))
        loads.append(pltpu.make_async_copy(cols_in.at[i], g_cols.at[i], sems.at[16 + i]))
    for load in loads:
        load.start()
    loads[0].wait()
    packed = [jnp.concatenate([small[i, 0], small[i, 1]], axis=1) for i in range(slots)]
    gain_total = packed[0][2:3]
    for block in packed[1:]:
        gain_total = gain_total + block[2:3]
    gain_v[...] = gain_total
    features = rows_of(
        *[jnp.concatenate([small[i, 0, 3:4], small[i, 0, 4:5]], axis=1) for i in range(slots)]
    )
    d_rows = rows_of(*[jnp.concatenate([block[0:1], block[1:2]], axis=1) for block in packed])
    emb_v[...] = jnp.dot(
        features.T, d_rows, precision=lax.Precision.HIGHEST, preferred_element_type=F32
    )
    copies = [
        pltpu.make_async_copy(gain_v, gain_out, sems.at[9]),
        pltpu.make_async_copy(emb_v, emb_out.at[0], sems.at[10]),
    ]
    for copy in copies:
        copy.start()
    for load in loads[1:]:
        load.wait()
    left = jnp.concatenate([act_t[i] for i in range(slots)], axis=1)
    for ky in range(3):
        for kx in range(3):
            rows, lanes = slice(ky * COLS, ky * COLS + PIX), slice(kx * C, (kx + 1) * C)
            right = jnp.concatenate([g_cols[i, rows, lanes] for i in range(slots)], axis=0)
            total = jnp.dot(left, right, preferred_element_type=F32)
            tap = ky * 3 + kx
            taps[tap] = total
            copy = pltpu.make_async_copy(taps.at[tap], conv_out.at[0, 2 - ky, 2 - kx], sems.at[tap])
            copy.start()
            copies.append(copy)
    for copy in copies:
        copy.wait()


def per_device(images, steps, out_grad, conv_weight, gn_gain, emb_weight):
    n_dp = lax.axis_size("dp")
    n_sec = lax.axis_size("section")
    flips = (1, 2, 3) if n_dp == 2 else (2,)
    half = C // 2
    freqs = np.exp(-math.log(10000.0) * np.arange(half, dtype=np.float32) / half)
    hbm = pl.BlockSpec(memory_space=pltpu.HBM)
    padded = PIX + 2 * COLS
    chain = pl.pallas_call(
        functools.partial(chain_body, n_sec, flips),
        out_shape=(
            jax.ShapeDtypeStruct((4, C, PIX), BF16),
            jax.ShapeDtypeStruct((4, padded, 3 * C), BF16),
            jax.ShapeDtypeStruct((4, 2, 8, HALF), F32),
        ),
        in_specs=[hbm] * 7,
        out_specs=(hbm, hbm, hbm),
        scratch_shapes=[
            pltpu.VMEM((4, C, PIX), BF16),
            pltpu.VMEM((4, padded, 3 * C), BF16),
            pltpu.VMEM((4, 2, 8, HALF), F32),
            pltpu.VMEM((PIX, HALF), BF16),
            pltpu.VMEM((PIX, HALF), BF16),
            pltpu.VMEM((PIX, HALF), BF16),
            pltpu.VMEM((PIX, HALF), BF16),
            pltpu.VMEM((PIX, HALF), BF16),
            pltpu.VMEM((2, PIX, HALF), BF16),
            pltpu.VMEM((4, 2, PIX, HALF), BF16),
            pltpu.VMEM((3, 3, C, HALF), BF16),
            pltpu.VMEM((3, 3, HALF, C), BF16),
            pltpu.VMEM((3, 3, C, HALF), BF16),
            pltpu.VMEM((padded, 3 * C), BF16),
            pltpu.VMEM((PIX, HALF), F32),
            pltpu.VMEM((PIX, HALF), F32),
            pltpu.VMEM((PIX, HALF), F32),
            pltpu.SMEM((2,), jnp.int32),
            pltpu.VMEM((1, HALF), F32),
            pltpu.VMEM((1, HALF), F32),
            pltpu.VMEM((2, C, HALF), BF16),
            pltpu.SemaphoreType.DMA((28,)),
            pltpu.SemaphoreType.DMA((28,)),
            pltpu.SemaphoreType.DMA((8,)),
            pltpu.SemaphoreType.DMA((9,)),
            pltpu.SemaphoreType.REGULAR,
        ],
        compiler_params=pltpu.CompilerParams(
            collective_id=0, has_side_effects=True, vmem_limit_bytes=56 * 1024 * 1024
        ),
    )(
        steps, jnp.asarray(freqs, F32)[None, :], images, out_grad, conv_weight, gn_gain, emb_weight
    )
    grads = pl.pallas_call(
        functools.partial(grad_body, 4 if n_dp == 2 else 2),
        out_shape=(
            jax.ShapeDtypeStruct((1, 3, 3, C, C), F32),
            jax.ShapeDtypeStruct((1, C), F32),
            jax.ShapeDtypeStruct((1, C, 2 * C), F32),
        ),
        in_specs=[hbm] * 3,
        out_specs=(hbm, hbm, hbm),
        scratch_shapes=[
            pltpu.VMEM((4, C, PIX), BF16),
            pltpu.VMEM((4, padded, 3 * C), BF16),
            pltpu.VMEM((4, 2, 8, HALF), F32),
            pltpu.VMEM((9, C, C), F32),
            pltpu.VMEM((1, C), F32),
            pltpu.VMEM((C, 2 * C), F32),
            pltpu.SemaphoreType.DMA((20,)),
        ],
        compiler_params=pltpu.CompilerParams(vmem_limit_bytes=56 * 1024 * 1024),
    )(*chain)
    if n_dp != 2:
        grads = lax.psum(grads, "dp")
    return grads


def solution(mesh):
    in_specs = (
        P("dp", "space", None, None),
        P("dp"),
        P("dp", "space", None, None),
        P("section", None, None, None, None),
        P("section", None),
        P("section", None, None),
    )
    out_specs = (P("section", None, None, None, None), P("section", None), P("section", None, None))
    return jax.shard_map(
        per_device, mesh=mesh, in_specs=in_specs, out_specs=out_specs, check_vma=False
    )
```
